128 devices in a mesh: pair: 8 (over z, core), ri: 16 (over y, x).
Axes of the slice: x: 4, y: 4, z: 4, core: 2. Of those that a mesh axis runs over, the one named last changes fastest.
Arguments:
- integrals: bfloat16 [128, 5, 144, 128, 128], P('pair', None, 'ri'), may hold values from -0.23632812 to 0.23632812
- lam_index: int32 [128, 5], P('pair'), may hold values from 0 to 127, as said below
- tile_count: int32 [128], P('pair'), may hold values from 1 to 5
- screen: int32 [128, 5], P('pair'), may hold values 0 or 1
- coefficients: bfloat16 [128, 16384], P(None, ('pair', 'ri')), may hold values from -0.52734375 to 0.52734375
- metric: bfloat16 [144, 144], replicated, may hold values from -0.5 to 0.5
Outputs:
- exchange: float32 [16384, 2048], P(('pair', 'ri'))
The draws below stay inside these ranges and needn't reach their ends.
Inputs may be any that keep to these rules, and one draw needn't show every extreme that they name: `lam_index`: slot 0 of block b names b itself; the partners of one block are distinct and lie ahead of it, cyclically, within 128 blocks.
All inputs are finite; a program needn't handle non-finite values. No bound on the sum of `screen` on one device may be relied on, other than what follows from the above.
Results may differ from the reference program's by a relative error of at most 0.0022.
Values may be sent and summed in bfloat16 or wider, within the bound.
No kernel may reach another device: no remote copies, remote signals or barrier semaphores. Data moves between devices by JAX's collectives and lax.ppermute only.
A program may use at most 256 MiB of HBM per device.

```python
import jax
import jax.numpy as jnp
from jax import lax

BS = 128
SLOTS = 5
OCC = 128
NBLK = 128
NORB = 16384
GROUP = 2048
NQ = 144
N_PAIR = 8


def draw_lam_index(key, part):
    key = jax.random.fold_in(key, 11)
    strides = jax.random.randint(key, (NBLK, SLOTS), 1, max(3, NBLK // SLOTS))
    reach = jnp.cumsum(strides, axis=1) - strides[:, :1]
    base_block = jnp.arange(NBLK, dtype=jnp.int32)[:, None]
    return ((base_block + reach) % NBLK).astype(jnp.int32)


def draw_tile_count(key, part):
    key = jax.random.fold_in(key, 12)
    counts = jax.random.randint(key, (NBLK,), 1, SLOTS + 1)
    position = jnp.arange(NBLK, dtype=jnp.int32)
    counts = jnp.where(position == 0, SLOTS, counts)
    counts = jnp.where(position == 1, 1, counts)
    return counts.astype(jnp.int32)


def with_ends(values, own_key, low, top_value):
    place = [jax.random.randint(jax.random.fold_in(own_key, axis), (), 0, length) for axis, length in enumerate(values.shape)]
    widest = values.shape.index(max(values.shape))
    neighbour = place[:widest] + [(place[widest] + 1) % values.shape[widest]] + place[widest + 1:]
    return values.at[tuple(place)].set(low).at[tuple(neighbour)].set(top_value)


def shard_levels(key, extent, split, least, high):
    def one(dim, parts):
        draws = jax.random.uniform(jax.random.fold_in(jax.random.fold_in(key, 6), dim), (parts,), jnp.float32, least / len(split), high / len(split))
        return jnp.repeat(jnp.exp(draws), extent[dim] // parts).reshape((-1,) + (1,) * (len(extent) - dim - 1))

    factor_of = one(*split[0])
    for cut in split[1:]:
        factor_of = factor_of * one(*cut)
    return factor_of


def scatter_about(own_key, extent, scale, limit, pieces=(), kind=jnp.bfloat16):
    drawn = scale * jax.random.normal(own_key, extent, jnp.float32)
    if pieces:
        drawn = drawn * shard_levels(own_key, extent, pieces, -0.22, 0.18)
    return jnp.clip(drawn, -limit, limit).astype(kind)


def setup_inputs(seed: int = 0) -> dict:
    key_of = jax.random.split(jax.random.key(seed), 7)
    return {
        "integrals": scatter_about(key_of[0], (NBLK, SLOTS, NQ, BS, BS), ((SLOTS * BS) ** -0.5), 0.23632812, ((0, 8), (2, 16))),
        "lam_index": draw_lam_index(jax.random.fold_in(key_of[6], 71), 0),
        "tile_count": draw_tile_count(jax.random.fold_in(key_of[6], 71), 0),
        "screen": with_ends((jax.random.randint(key_of[3], (NBLK, SLOTS), 0, 4) < 3).astype(jnp.int32), jax.random.fold_in(key_of[3], 1), 0, 1),
        "coefficients": scatter_about(key_of[4], (OCC, NORB), (OCC ** -0.5), 0.52734375, ((1, 128),)),
        "metric": scatter_about(key_of[5], (NQ, NQ), NQ ** -0.5, 0.5),
    }


def reference(integrals, lam_index, tile_count, screen, coefficients, metric):
    slot_ids = jnp.arange(SLOTS, dtype=jnp.int32)
    kept_slot = jnp.where((slot_ids[None, :] < tile_count[:, None]) & (screen > 0), 1.0, 0.0).astype(jnp.float32)
    coef_blocks = coefficients.reshape(OCC, NBLK, BS)
    picked = coef_blocks[:, lam_index]
    picked = (picked.astype(jnp.float32) * kept_slot[None, :, :, None]).astype(jnp.bfloat16)
    picked = jnp.transpose(picked, (1, 0, 2, 3))

    def block_term(inputs):
        tiles, coef_slots = inputs
        return jnp.einsum("sqml,osl->oqm", tiles.astype(jnp.float32), coef_slots.astype(jnp.float32))

    fitted_blocks = lax.map(block_term, (integrals, picked)).astype(jnp.bfloat16)
    fitted = jnp.transpose(fitted_blocks, (1, 2, 0, 3)).reshape(OCC, NQ, NORB)
    factors = jnp.einsum("pq,oqn->opn", metric.astype(jnp.float32), fitted.astype(jnp.float32)).astype(jnp.bfloat16)
    grouped = jnp.transpose(factors.reshape(OCC, NQ, N_PAIR, GROUP), (2, 0, 1, 3))

    def group_term(group_factors):
        values = group_factors.astype(jnp.float32)
        return jnp.einsum("opm,opn->mn", values, values)

    exchange = lax.map(group_term, grouped)
    return exchange.reshape(NORB, GROUP)
```

```python
import jax
import jax.numpy as jnp
from jax import lax
from jax.experimental import pallas as pl
from jax.experimental.pallas import tpu as pltpu
from jax.sharding import PartitionSpec as P

VMEM_LIMIT = 56 * 1024 * 1024
NT = (((1,), (1,)), ((), ()))


def fit_kernel(lam, kept, coefs, low_tiles, high_tiles, out, picked):
    slots, own_q, size = low_tiles.shape[1:4]
    ri = coefs.shape[0]
    owners, share = out.shape[0], out.shape[2] // 2
    step, steps = pl.program_id(0), pl.num_programs(0)
    for half, tiles in enumerate((low_tiles, high_tiles)):
        for s in range(slots):
            at = (step + half * steps) * slots + s
            block = lam[at]
            tile = coefs[lax.rem(block, ri), lax.div(block, ri)]
            picked[half, :, s * size:(s + 1) * size] = jnp.where(kept[at] > 0, tile, jnp.zeros_like(tile))
    for q in range(own_q):
        parts = []
        for half, tiles in enumerate((low_tiles, high_tiles)):
            wide = jnp.concatenate([tiles[0, s, q] for s in range(slots)], axis=1)
            value = lax.dot_general(picked[half], wide, NT, preferred_element_type=jnp.float32)
            parts.append(value.reshape(owners, share, size))
        out[:, q] = jnp.concatenate(parts, axis=1).astype(out.dtype)


def fit(integrals, lam, kept, coefs):
    blocks, slots, own_q, size, _ = integrals.shape
    occupied = coefs.shape[2]
    ri = coefs.shape[0]
    share = occupied // ri
    steps = blocks // 2
    tile_block = (1, slots, own_q, size, size)
    return pl.pallas_call(
        fit_kernel,
        grid_spec=pltpu.PrefetchScalarGridSpec(
            num_scalar_prefetch=2,
            grid=(steps,),
            in_specs=[
                pl.BlockSpec(coefs.shape, lambda i, *_: (0, 0, 0, 0)),
                pl.BlockSpec(tile_block, lambda i, *_: (i, 0, 0, 0, 0)),
                pl.BlockSpec(tile_block, lambda i, *_: (i + steps, 0, 0, 0, 0)),
            ],
            out_specs=pl.BlockSpec((ri, own_q, 2 * share, size), lambda i, *_: (0, 0, 0, i)),
            scratch_shapes=[pltpu.VMEM((2, occupied, slots * size), jnp.bfloat16)],
        ),
        out_shape=jax.ShapeDtypeStruct((ri, own_q, 2 * share, steps * size), jnp.bfloat16),
        compiler_params=pltpu.CompilerParams(vmem_limit_bytes=VMEM_LIMIT),
        name="fit",
    )(lam, kept, coefs, integrals, integrals)


def exchange_kernel(metric, fitted, out, wide, factors, turned):
    ri, own_q, rows, half_cols = fitted.shape
    share = rows // 2
    n_q = metric.shape[0]
    lanes = wide.shape[1]
    tile = wide.shape[3]
    chunk = lanes * tile
    size = out.shape[1]

    @pl.when(pl.program_id(0) == 0)
    def _():
        def one(c, _):
            base = pl.multiple_of(c * chunk, chunk)
            for k in range(own_q):
                x = fitted[:, k, :, pl.ds(base, chunk)].astype(jnp.float32)
                for h in range(2):
                    y = x[:, h * share:(h + 1) * share, :].reshape(ri * share, chunk)
                    for t in range(lanes):
                        wide[h, t, k * ri * share:(k + 1) * ri * share, :] = y[:, t * tile:(t + 1) * tile]
            for h in range(2):
                at = pl.multiple_of(base + h * half_cols, chunk)
                parts = []
                for o in range(share):
                    x = jnp.concatenate(
                        [wide[h, t, pl.ds(o, n_q, stride=share), :] for t in range(lanes)], axis=1
                    ).astype(jnp.bfloat16)
                    y = jnp.dot(metric[...], x, preferred_element_type=jnp.float32).astype(jnp.bfloat16)
                    parts.append(y)
                whole = jnp.concatenate(parts, axis=0)
                factors[:, pl.ds(at, chunk)] = whole
                if h == 0:
                    factors[:, pl.ds(pl.multiple_of(base + 2 * half_cols, chunk), chunk)] = whole
                turned[pl.ds(at, chunk), :] = whole.T
            return 0

        lax.fori_loop(0, half_cols // chunk, one, 0)

    pair = 2 * size
    span = out.shape[2]
    start = pl.multiple_of(pl.program_id(0) * pair, pair)
    value = jnp.dot(
        turned[pl.ds(start, pair), :],
        factors[:, pl.ds(start, span + size)],
        preferred_element_type=jnp.float32,
    ).astype(out.dtype)
    out[0] = value[:size, :span]
    out[1] = value[size:, size:]


def exchange_panels(metric, fitted):
    ri, own_q, rows, half_cols = fitted.shape
    cols = 2 * half_cols
    size = cols // ri
    span = (ri // 2 + 1) * size
    depth = own_q * ri * rows // 2
    return pl.pallas_call(
        exchange_kernel,
        grid=(ri // 2,),
        in_specs=[
            pl.BlockSpec(metric.shape, lambda i: (0, 0)),
            pl.BlockSpec(fitted.shape, lambda i: (0, 0, 0, 0)),
        ],
        out_specs=pl.BlockSpec((2, size, span), lambda i: (i, 0, 0)),
        out_shape=jax.ShapeDtypeStruct((ri, size, span), jnp.bfloat16),
        scratch_shapes=[
            pltpu.VMEM((2, 2, depth, size), jnp.float32),
            pltpu.VMEM((depth, cols + half_cols), jnp.bfloat16),
            pltpu.VMEM((cols, depth), jnp.bfloat16),
        ],
        compiler_params=pltpu.CompilerParams(vmem_limit_bytes=VMEM_LIMIT),
        name="exchange_panels",
    )(metric, fitted)


def sum_kernel(parts, own, mirror):
    total = parts[0].astype(jnp.float32)
    for s in range(1, parts.shape[0]):
        total = total + parts[s].astype(jnp.float32)
    own[...] = total
    mirror[0] = total.T.astype(mirror.dtype)


def sum_panels(parts):
    ri, size, span = parts.shape
    blocks = span // size
    return pl.pallas_call(
        sum_kernel,
        grid=(blocks,),
        in_specs=[pl.BlockSpec((ri, size, size), lambda d: (0, 0, d))],
        out_specs=[
            pl.BlockSpec((size, size), lambda d: (0, d)),
            pl.BlockSpec((1, size, size), lambda d: (d, 0, 0)),
        ],
        out_shape=[
            jax.ShapeDtypeStruct((size, span), jnp.float32),
            jax.ShapeDtypeStruct((blocks, size, size), jnp.bfloat16),
        ],
        name="sum_panels",
    )(parts)


def place_kernel(me, own, *rest):
    mirrors, out = rest[:-1], rest[-1]
    size = own.shape[0]
    ri = out.shape[1] // size
    for d in range(own.shape[1] // size):
        at = lax.rem(me[0] + d, ri) * size
        out[:, pl.ds(pl.multiple_of(at, size), size)] = own[:, d * size:(d + 1) * size]
    for d, mirror in enumerate(mirrors, 1):
        at = lax.rem(me[0] + ri - d, ri) * size
        out[:, pl.ds(pl.multiple_of(at, size), size)] = mirror[...].astype(out.dtype)


def place(me, own, mirrors):
    size = own.shape[0]
    ri = len(mirrors) * 2 + 2
    return pl.pallas_call(
        place_kernel,
        in_specs=[pl.BlockSpec(memory_space=pltpu.SMEM)] + [pl.BlockSpec(memory_space=pltpu.VMEM)] * (1 + len(mirrors)),
        out_specs=pl.BlockSpec(memory_space=pltpu.VMEM),
        out_shape=jax.ShapeDtypeStruct((size, ri * size), jnp.float32),
        name="place",
    )(me, own, *mirrors)


def body(integrals, lam_index, tile_count, screen, coefficients, metric):
    slots = integrals.shape[1]
    own_q = integrals.shape[2]
    ri = lax.axis_size("ri")
    slot_ids = jnp.arange(slots, dtype=jnp.int32)
    kept = ((slot_ids[None, :] < tile_count[:, None]) & (screen > 0)).astype(jnp.int32).reshape(-1)
    coefs = lax.all_gather(lax.all_gather(coefficients, "pair", axis=0), "ri", axis=0)
    mine = fit(integrals, lam_index.reshape(-1), kept, coefs)
    fitted = lax.all_to_all(mine, "ri", 0, 0)
    n_q = metric.shape[0]
    by_step = metric.reshape(n_q, ri, own_q).transpose(0, 2, 1).reshape(n_q, n_q)
    panels = exchange_panels(by_step, fitted)
    own, mirror = sum_panels(lax.all_to_all(panels, "ri", 0, 0))
    mirrors = [
        lax.ppermute(mirror[d], "ri", [(i, (i + d) % ri) for i in range(ri)])
        for d in range(1, ri // 2)
    ]
    me = lax.axis_index("ri").astype(jnp.int32).reshape(1)
    return place(me, own, mirrors)


def solution(mesh):
    placed = (
        P("pair", None, "ri", None, None),
        P("pair", None),
        P("pair"),
        P("pair", None),
        P(None, ("pair", "ri")),
        P(),
    )
    return jax.shard_map(
        body, mesh=mesh, in_specs=placed, out_specs=P(("pair", "ri"), None), check_vma=False
    )
```

```python
import functools

import jax
import jax.numpy as jnp
from jax import lax
from jax.experimental import pallas as pl
from jax.experimental.pallas import tpu as pltpu
from jax.sharding import PartitionSpec as P

VMEM_LIMIT = 56 * 1024 * 1024
NT = (((1,), (1,)), ((), ()))
SIDE = 4
HALVES = 2
ON_VMEM = pl.BlockSpec(memory_space=pltpu.VMEM)
ON_SMEM = pl.BlockSpec(memory_space=pltpu.SMEM)


class Table:
    def __init__(self, blocks, slots):
        self.blocks, self.slots = blocks, slots
        self.count = 0
        self.pick = self.count + blocks
        self.row = self.pick + blocks * slots
        self.slot = self.row + blocks * slots
        self.ri = self.slot + blocks * slots
        self.x, self.y, self.core = self.ri + 1, self.ri + 2, self.ri + 3
        self.size = self.ri + 4


def prepare_kernel(at, place, lam, tile_count, screen, own, table, copies):
    for n in range(copies.shape[0]):
        copies[n] = own[...]
    for n in range(4):
        table[at.ri + n] = place[n]

    def one(b, _):
        count = jnp.int32(0)
        base = b * at.slots
        before = jnp.maximum(base - at.slots, 0)
        for s in range(at.slots):
            first = lax.rem(b, at.blocks // HALVES) == 0
            table[at.pick + base + s] = 0
            table[at.row + base + s] = jnp.where(first, b, table[at.row + before + s])
            table[at.slot + base + s] = jnp.where(first, s, table[at.slot + before + s])
        for s in range(at.slots):
            keep = jnp.logical_and(s < tile_count[b], screen[b, s] > 0)

            @pl.when(keep)
            def _():
                table[at.pick + base + count] = lam[b, s]
                table[at.row + base + count] = b
                table[at.slot + base + count] = s

            count = count + keep.astype(jnp.int32)
        table[at.count + b] = count
        return 0

    lax.fori_loop(0, at.blocks, one, 0)


def prepare(at, place, lam, tile_count, screen, own):
    return pl.pallas_call(
        functools.partial(prepare_kernel, at),
        in_specs=[ON_SMEM] * 4 + [ON_VMEM],
        out_specs=[ON_SMEM, ON_VMEM],
        out_shape=[
            jax.ShapeDtypeStruct((at.size,), jnp.int32),
            jax.ShapeDtypeStruct((SIDE,) + own.shape, own.dtype),
        ],
        name="prepare",
    )(place, lam, tile_count, screen, own)


def fit_kernel(at, table, same, other, *rest):
    slots = at.slots
    tiles, (out, picked, total) = rest[: HALVES * slots], rest[HALVES * slots:]
    ri = same.shape[0]
    own_q, size = out.shape[1], out.shape[3]
    share = out.shape[2] // HALVES
    step, steps = pl.program_id(0), pl.num_programs(0)
    for half in range(HALVES):
        block = step + half * steps
        count = table[at.count + block]

        @pl.when(count == 0)
        def _():
            total[half] = jnp.zeros(total.shape[1:], total.dtype)

        for s in range(0, slots, 2):
            pair = range(s, min(s + 2, slots))

            @pl.when(count > s)
            def _():
                for n, j in enumerate(pair):
                    name = table[at.pick + block * slots + j]
                    row, part = lax.rem(name, ri), lax.div(name, ri)
                    z, core = lax.div(part, 2), lax.rem(part, 2)
                    tile = jnp.where(core == table[at.core], same[row, z], other[row, z])
                    tile = jnp.where(j < count, tile, jnp.zeros_like(tile))
                    picked[half, :, n * size:(n + 1) * size] = tile
                depth = len(pair) * size
                wide = [tiles[half * slots + j][0, 0].reshape(own_q * size, size) for j in pair]
                wide = jnp.concatenate(wide, axis=1) if len(wide) > 1 else wide[0]
                value = lax.dot_general(picked[half, :, :depth], wide, NT, preferred_element_type=jnp.float32)
                total[half] = value if s == 0 else total[half] + value

    for q in range(own_q):
        parts = [
            total[half, :, q * size:(q + 1) * size].reshape(ri, share, size) for half in range(HALVES)
        ]
        out[:, q] = jnp.concatenate(parts, axis=1).astype(out.dtype)


def fit(at, table, integrals, same, other):
    blocks, slots, own_q, size, _ = integrals.shape
    ri, _, occupied, _ = same.shape
    share = occupied // ri
    steps = blocks // HALVES

    def place(half, j):
        def index(i, table):
            n = (i + half * steps) * slots + j
            return table[at.row + n], table[at.slot + n], 0, 0, 0

        return pl.BlockSpec((1, 1, own_q, size, size), index)

    whole = pl.BlockSpec(same.shape, lambda i, table: (0, 0, 0, 0))
    return pl.pallas_call(
        functools.partial(fit_kernel, at),
        grid_spec=pltpu.PrefetchScalarGridSpec(
            num_scalar_prefetch=1,
            grid=(steps,),
            in_specs=[whole, whole] + [place(half, j) for half in range(HALVES) for j in range(slots)],
            out_specs=pl.BlockSpec((ri, own_q, HALVES * share, size), lambda i, table: (0, 0, 0, i)),
            scratch_shapes=[
                pltpu.VMEM((HALVES, occupied, 2 * size), jnp.bfloat16),
                pltpu.VMEM((HALVES, occupied, own_q * size), jnp.float32),
            ],
        ),
        out_shape=jax.ShapeDtypeStruct((ri, own_q, HALVES * share, steps * size), jnp.bfloat16),
        compiler_params=pltpu.CompilerParams(vmem_limit_bytes=VMEM_LIMIT),
        name="fit",
    )(table, same, other, *[integrals] * (HALVES * slots))


def exchange_kernel(at, table, metric, fitted, *rest):
    by_x, by_y = rest[:SIDE], rest[SIDE:2 * SIDE]
    wide, factors, turned = rest[2 * SIDE:]
    ri, own_q, rows, half_cols = fitted.shape
    share = rows // HALVES
    n_q = metric.shape[0]
    lanes, tile = wide.shape[1], wide.shape[3]
    chunk = lanes * tile

    def one(c, _):
        base = pl.multiple_of(c * chunk, chunk)
        for k in range(own_q):
            x = fitted[:, k, :, pl.ds(base, chunk)].astype(jnp.float32)
            for r in range(ri):
                to = (r * own_q + k) * share
                for h in range(HALVES):
                    for t in range(lanes):
                        wide[h, t, to:to + share, :] = x[r, h * share:(h + 1) * share, t * tile:(t + 1) * tile]
        for h in range(HALVES):
            start = pl.multiple_of(base + h * half_cols, chunk)
            parts = []
            for o in range(share):
                x = jnp.concatenate(
                    [wide[h, t, pl.ds(o, n_q, stride=share), :] for t in range(lanes)], axis=1
                ).astype(jnp.bfloat16)
                parts.append(jnp.dot(metric[...], x, preferred_element_type=jnp.float32).astype(jnp.bfloat16))
            whole = jnp.concatenate(parts, axis=0)
            factors[:, pl.ds(start, chunk)] = whole
            if h == 0:
                factors[:, pl.ds(pl.multiple_of(base + HALVES * half_cols, chunk), chunk)] = whole
            turned[pl.ds(start, chunk), :] = whole.T
        return 0

    lax.fori_loop(0, half_cols // chunk, one, 0)

    _, cut, span = by_x[0].shape
    size = 2 * cut

    def panels(n, _):
        start = pl.multiple_of(n * 2 * size, 2 * size)
        value = jnp.dot(
            turned[pl.ds(start, 2 * size), :],
            factors[:, pl.ds(start, span + size)],
            preferred_element_type=jnp.float32,
        ).astype(jnp.bfloat16)
        y = lax.div(n, SIDE // 2)
        for side in range(2):
            x = 2 * lax.rem(n, SIDE // 2) + side
            panel = value[side * size:(side + 1) * size, side * size:side * size + span]
            step_x = lax.rem(x + SIDE - table[at.x], SIDE)
            step_y = lax.rem(y + SIDE - table[at.y], SIDE)
            for k in range(SIDE):
                @pl.when(step_x == k)
                def _():
                    by_x[k][y] = panel[:cut]

                @pl.when(step_y == k)
                def _():
                    by_y[k][x] = panel[cut:]
        return 0

    lax.fori_loop(0, ri // 2, panels, 0)


def exchange_panels(at, table, metric, fitted):
    ri, own_q, rows, half_cols = fitted.shape
    cols = HALVES * half_cols
    size = cols // ri
    span = (ri // 2 + 1) * size
    depth = own_q * ri * rows // HALVES
    return pl.pallas_call(
        functools.partial(exchange_kernel, at),
        in_specs=[ON_SMEM, ON_VMEM, ON_VMEM],
        out_specs=[ON_VMEM] * (2 * SIDE),
        out_shape=[jax.ShapeDtypeStruct((SIDE, size // 2, span), jnp.bfloat16)] * (2 * SIDE),
        scratch_shapes=[
            pltpu.VMEM((HALVES, 2, depth, size), jnp.float32),
            pltpu.VMEM((depth, cols + half_cols), jnp.bfloat16),
            pltpu.VMEM((cols, depth), jnp.bfloat16),
        ],
        compiler_params=pltpu.CompilerParams(vmem_limit_bytes=VMEM_LIMIT),
        name="exchange_panels",
    )(table, metric, fitted)


def first_sum_kernel(at, table, *rest):
    ins, outs = rest[:2 * SIDE], rest[2 * SIDE:]
    for path, mine in enumerate((table[at.y], table[at.x])):
        for k in range(SIDE):
            to = lax.rem(mine + k, SIDE)
            total = ins[path * SIDE][to].astype(jnp.float32)
            for j in range(1, SIDE):
                total = total + ins[path * SIDE + j][to].astype(jnp.float32)
            out = outs[path * SIDE + k]
            out[...] = total.astype(out.dtype)


def first_sum(at, table, parts):
    shape = parts[0].shape[1:]
    return pl.pallas_call(
        functools.partial(first_sum_kernel, at),
        in_specs=[ON_SMEM] + [ON_VMEM] * len(parts),
        out_specs=[ON_VMEM] * len(parts),
        out_shape=[
            jax.ShapeDtypeStruct(shape, jnp.float32 if n % SIDE == 0 else jnp.bfloat16)
            for n in range(len(parts))
        ],
        compiler_params=pltpu.CompilerParams(vmem_limit_bytes=VMEM_LIMIT),
        name="first_sum",
    )(table, *parts)


def second_sum_kernel(*refs):
    ins, own, mirrors = refs[:2 * SIDE], refs[2 * SIDE], refs[2 * SIDE + 1:]
    cut = ins[0].shape[0]
    size = 2 * cut
    for path in range(2):
        total = ins[path * SIDE][...]
        for j in range(1, SIDE):
            total = total + ins[path * SIDE + j][...].astype(jnp.float32)
        own[path * cut:(path + 1) * cut, :] = total
    for d, mirror in enumerate(mirrors, 1):
        mirror[...] = own[:, d * size:(d + 1) * size].T.astype(mirror.dtype)


def second_sum(parts):
    cut, span = parts[0].shape
    size = 2 * cut
    mirrors = span // size - 2
    return pl.pallas_call(
        second_sum_kernel,
        in_specs=[ON_VMEM] * len(parts),
        out_specs=[ON_VMEM] * (1 + mirrors),
        out_shape=[jax.ShapeDtypeStruct((size, span), jnp.float32)]
        + [jax.ShapeDtypeStruct((size, size), jnp.bfloat16)] * mirrors,
        compiler_params=pltpu.CompilerParams(vmem_limit_bytes=VMEM_LIMIT),
        name="second_sum",
    )(*parts)


def place_kernel(at, table, own, *rest):
    mirrors, out = rest[:-1], rest[-1]
    size = own.shape[0]
    ri = out.shape[1] // size
    for d in range(own.shape[1] // size):
        to = lax.rem(table[at.ri] + d, ri) * size
        out[:, pl.ds(pl.multiple_of(to, size), size)] = own[:, d * size:(d + 1) * size]
    for d, mirror in enumerate(mirrors, 1):
        to = lax.rem(table[at.ri] + ri - d, ri) * size
        out[:, pl.ds(pl.multiple_of(to, size), size)] = mirror[...].astype(out.dtype)


def place_blocks(at, table, own, mirrors):
    size = own.shape[0]
    ri = len(mirrors) * 2 + 2
    return pl.pallas_call(
        functools.partial(place_kernel, at),
        in_specs=[ON_SMEM] + [ON_VMEM] * (1 + len(mirrors)),
        out_specs=ON_VMEM,
        out_shape=jax.ShapeDtypeStruct((size, ri * size), jnp.float32),
        name="place_blocks",
    )(table, own, *mirrors)


def along_x(k):
    return [(y * SIDE + x, y * SIDE + (x + k) % SIDE) for y in range(SIDE) for x in range(SIDE)]


def along_y(k):
    return [(y * SIDE + x, (y + k) % SIDE * SIDE + x) for y in range(SIDE) for x in range(SIDE)]


def body(integrals, lam_index, tile_count, screen, coefficients, metric):
    ri, pairs = lax.axis_size("ri"), lax.axis_size("pair")
    at = Table(*integrals.shape[:2])
    here = lax.axis_index("ri").astype(jnp.int32)
    core = lax.rem(lax.axis_index("pair").astype(jnp.int32), 2)
    place = jnp.stack([here, lax.rem(here, SIDE), lax.div(here, SIDE), core])
    table, copies = prepare(at, place, lam_index, tile_count, screen, coefficients)

    one_core = [list(range(c, pairs, 2)) for c in range(2)]
    column = lax.all_to_all(copies, "pair", 0, 0, axis_index_groups=one_core, tiled=True)
    column = jnp.broadcast_to(column[None], (ri,) + column.shape)
    same = lax.all_to_all(column, "ri", 0, 0, tiled=True)
    other = lax.ppermute(same, "pair", [(p, p ^ 1) for p in range(pairs)])

    mine = fit(at, table, integrals, same, other)
    fitted = lax.all_to_all(mine, "ri", 0, 0, tiled=True)
    panels = exchange_panels(at, table, metric, fitted)

    def exchange_two(parts, first, second):
        return (
            parts[:1] + [lax.ppermute(parts[k], "ri", first(k)) for k in range(1, SIDE)]
            + parts[SIDE:SIDE + 1] + [lax.ppermute(parts[SIDE + k], "ri", second(k)) for k in range(1, SIDE)]
        )

    sums = first_sum(at, table, exchange_two(list(panels), along_x, along_y))
    own, *mirrors = second_sum(exchange_two(list(sums), along_y, along_x))
    mirrors = [
        lax.ppermute(mirror, "ri", [(i, (i + d) % ri) for i in range(ri)])
        for d, mirror in enumerate(mirrors, 1)
    ]
    return place_blocks(at, table, own, mirrors)


def solution(mesh):
    placed = (
        P("pair", None, "ri", None, None),
        P("pair", None),
        P("pair"),
        P("pair", None),
        P(None, ("pair", "ri")),
        P(),
    )
    return jax.shard_map(
        body, mesh=mesh, in_specs=placed, out_specs=P(("pair", "ri"), None), check_vma=False
    )
```

```python
import functools

import jax
import jax.numpy as jnp
from jax import lax
from jax.experimental import pallas as pl
from jax.experimental.pallas import tpu as pltpu
from jax.sharding import PartitionSpec as P

MIB = 1024 * 1024
NT = (((1,), (1,)), ((), ()))
SIDE = 4
HALVES = 2
CHUNKS = 2
ON_VMEM = pl.BlockSpec(memory_space=pltpu.VMEM)
ON_SMEM = pl.BlockSpec(memory_space=pltpu.SMEM)


class Table:
    def __init__(self, blocks, slots):
        self.blocks, self.slots = blocks, slots
        self.count = 0
        self.slot = self.count + blocks
        self.core = self.slot + blocks * slots
        self.top = self.core + blocks * slots
        self.low = self.top + blocks * slots
        self.ri = self.low + blocks * slots
        self.x, self.y = self.ri + 1, self.ri + 2
        self.size = self.ri + 3


def prepare_kernel(at, place, lam, tile_count, screen, table):
    ri, x, y, z, core = (place[n] for n in range(5))
    for n in range(3):
        table[at.ri + n] = place[n]

    def one(b, _):
        count = jnp.int32(0)
        for s in range(at.slots):
            keep = jnp.logical_and(s < tile_count[b], screen[b, s] > 0)
            to = b * at.slots + count
            name = lam[b, s]

            part, place_ri = lax.div(name, SIDE * SIDE), lax.rem(name, SIDE * SIDE)
            back_x = lax.rem(x + SIDE - lax.rem(place_ri, SIDE), SIDE)
            back_y = lax.rem(y + SIDE - lax.div(place_ri, SIDE), SIDE)
            back_z = lax.rem(z + SIDE - lax.div(part, 2), SIDE)

            @pl.when(keep)
            def _():
                table[at.slot + to] = s
                table[at.core + to] = lax.rem(part + core, 2)
                table[at.top + to] = (back_y * SIDE + back_x) * SIDE + back_z
                table[at.low + to] = (back_x * SIDE + back_y) * SIDE + back_z

            count = count + keep.astype(jnp.int32)
        table[at.count + b] = count
        return 0

    lax.fori_loop(0, at.blocks, one, 0)


def prepare(at, place, lam, tile_count, screen):
    return pl.pallas_call(
        functools.partial(prepare_kernel, at),
        in_specs=[ON_SMEM] * 4,
        out_specs=ON_SMEM,
        out_shape=jax.ShapeDtypeStruct((at.size,), jnp.int32),
        name="prepare",
    )(place, lam, tile_count, screen)


def gather(coefficients):
    pairs = lax.axis_size("pair")
    half = coefficients.shape[0] // 2

    def around(value, axis, shift):
        return jnp.stack([value] + [lax.ppermute(value, axis, shift(k)) for k in range(1, SIDE)])

    column = around(coefficients, "pair", lambda k: [(p, (p + 2 * k) % pairs) for p in range(pairs)])
    top = around(around(column[:, :half], "ri", along_x), "ri", along_y)
    low = around(around(column[:, half:], "ri", along_y), "ri", along_x)
    same = jnp.stack([top, low]).reshape((2, SIDE ** 3) + top.shape[3:])
    return same, lax.ppermute(same, "pair", [(p, p ^ 1) for p in range(pairs)])


def fit_kernel(at, table, same, other, integrals, out, tiles, picked, total, done):
    slots = at.slots
    _, _, cut, size = same.shape
    ri, own_q, rows, _ = out.shape
    share = rows // HALVES
    steps = at.blocks // HALVES

    def copy(block, j):
        slot = table[at.slot + block * slots + j]
        return pltpu.make_async_copy(integrals.at[block, slot], tiles.at[block, j], done.at[block, j])

    def kept(block, act):
        for j in range(slots):
            @pl.when(j < table[at.count + block])
            def _():
                act(copy(block, j))

    def begin(step, _):
        for half in range(HALVES):
            kept(step + half * steps, lambda c: c.start())
        return 0

    lax.fori_loop(0, steps, begin, 0)

    def one(step, _):
        for half in range(HALVES):
            block = step + half * steps
            count = table[at.count + block]
            kept(block, lambda c: c.wait())

            @pl.when(count == 0)
            def _():
                total[half] = jnp.zeros(total.shape[1:], total.dtype)

            for c in range(1, slots + 1):
                @pl.when(count == c)
                def _():
                    for j in range(c):
                        n = block * slots + j
                        for part, start in enumerate((at.top, at.low)):
                            name = table[start + n]
                            tile = jnp.where(table[at.core + n] == 0, same[part, name], other[part, name])
                            picked[half, part * cut:(part + 1) * cut, j * size:(j + 1) * size] = tile
                    wide = [tiles[block, j].reshape(own_q * size, size) for j in range(c)]
                    wide = jnp.concatenate(wide, axis=1) if c > 1 else wide[0]
                    total[half] = lax.dot_general(
                        picked[half, :, :c * size], wide, NT, preferred_element_type=jnp.float32
                    )

        for q in range(own_q):
            parts = [
                total[half, :, q * size:(q + 1) * size].reshape(ri, share, size) for half in range(HALVES)
            ]
            out[:, q, :, pl.ds(pl.multiple_of(step * size, size), size)] = (
                jnp.concatenate(parts, axis=1).astype(out.dtype)
            )
        return 0

    lax.fori_loop(0, steps, one, 0)


def fit(at, table, integrals, same, other):
    blocks, slots, own_q, size, _ = integrals.shape
    occupied = 2 * same.shape[2]
    ri = SIDE * SIDE
    share = occupied // ri
    return pl.pallas_call(
        functools.partial(fit_kernel, at),
        in_specs=[ON_SMEM, ON_VMEM, ON_VMEM, pl.BlockSpec(memory_space=pl.ANY)],
        out_specs=ON_VMEM,
        scratch_shapes=[
            pltpu.VMEM((blocks, slots, own_q, size, size), jnp.bfloat16),
            pltpu.VMEM((HALVES, occupied, slots * size), jnp.bfloat16),
            pltpu.VMEM((HALVES, occupied, own_q * size), jnp.float32),
            pltpu.SemaphoreType.DMA((blocks, slots)),
        ],
        out_shape=jax.ShapeDtypeStruct((ri, own_q, HALVES * share, blocks // HALVES * size), jnp.bfloat16),
        compiler_params=pltpu.CompilerParams(vmem_limit_bytes=40 * MIB),
        cost_estimate=pl.CostEstimate(flops=3 * 10 ** 9, bytes_accessed=20 * 10 ** 6, transcendentals=0),
        name="fit",
    )(table, same, other, integrals)


def factor_kernel(metric, fitted, factors, turned, wide):
    ri, own_q, rows, half_cols = fitted.shape
    share = rows // HALVES
    n_q = metric.shape[0]
    lanes, tile = wide.shape[1], wide.shape[3]
    chunk = lanes * tile

    def one(c, _):
        base = pl.multiple_of(c * chunk, chunk)
        for k in range(own_q):
            x = fitted[:, k, :, pl.ds(base, chunk)].astype(jnp.float32)
            for r in range(ri):
                to = (r * own_q + k) * share
                for h in range(HALVES):
                    for t in range(lanes):
                        wide[h, t, to:to + share, :] = x[r, h * share:(h + 1) * share, t * tile:(t + 1) * tile]
        for h in range(HALVES):
            start = pl.multiple_of(base + h * half_cols, chunk)
            parts = []
            for o in range(share):
                x = jnp.concatenate(
                    [wide[h, t, pl.ds(o, n_q, stride=share), :] for t in range(lanes)], axis=1
                ).astype(jnp.bfloat16)
                parts.append(jnp.dot(metric[...], x, preferred_element_type=jnp.float32).astype(jnp.bfloat16))
            whole = jnp.concatenate(parts, axis=0)
            factors[:, pl.ds(start, chunk)] = whole
            if h == 0:
                factors[:, pl.ds(pl.multiple_of(base + HALVES * half_cols, chunk), chunk)] = whole
            turned[pl.ds(start, chunk), :] = whole.T
        return 0

    lax.fori_loop(0, half_cols // chunk, one, 0)


def factor(metric, fitted):
    ri, own_q, rows, half_cols = fitted.shape
    cols = HALVES * half_cols
    depth = own_q * ri * rows // HALVES
    return pl.pallas_call(
        factor_kernel,
        in_specs=[ON_VMEM] * 2,
        out_specs=[ON_VMEM] * 2,
        out_shape=[
            jax.ShapeDtypeStruct((depth, cols + half_cols), jnp.bfloat16),
            jax.ShapeDtypeStruct((cols, depth), jnp.bfloat16),
        ],
        scratch_shapes=[pltpu.VMEM((HALVES, 2, depth, cols // ri), jnp.float32)],
        compiler_params=pltpu.CompilerParams(vmem_limit_bytes=28 * MIB),
        cost_estimate=pl.CostEstimate(flops=2 * 10 ** 9, bytes_accessed=10 * 10 ** 6, transcendentals=0),
        name="factor",
    )(metric, fitted)


def panel_kernel(at, first, table, factors, turned, *rest):
    by_x, by_y, panels = rest[:SIDE], rest[SIDE:2 * SIDE], rest[2 * SIDE]
    ri, size, span = panels.shape
    cut = size // 2

    def two(n, _):
        start = pl.multiple_of(n * 2 * size, 2 * size)
        value = jnp.dot(
            turned[pl.ds(start, 2 * size), :],
            factors[:, pl.ds(start + first * size, span + size)],
            preferred_element_type=jnp.float32,
        ).astype(jnp.bfloat16)
        for side in range(2):
            panels[2 * n + side] = value[side * size:(side + 1) * size, side * size:side * size + span]
        return 0

    lax.fori_loop(0, ri // 2, two, 0)
    for k in range(SIDE):
        x = lax.rem(table[at.x] + k, SIDE)
        y = lax.rem(table[at.y] + k, SIDE)
        for j in range(SIDE):
            by_x[k][j] = panels[j * SIDE + x, :cut]
            by_y[k][j] = panels[y * SIDE + j, cut:]


def panel_columns(at, first, last, table, factors, turned):
    cols, depth = turned.shape
    size = cols // (SIDE * SIDE)
    span = (last - first) * size
    return pl.pallas_call(
        functools.partial(panel_kernel, at, first),
        in_specs=[ON_SMEM, ON_VMEM, ON_VMEM],
        out_specs=[ON_VMEM] * (2 * SIDE),
        out_shape=[jax.ShapeDtypeStruct((SIDE, size // 2, span), jnp.bfloat16)] * (2 * SIDE),
        scratch_shapes=[pltpu.VMEM((SIDE * SIDE, size, span), jnp.bfloat16)],
        compiler_params=pltpu.CompilerParams(vmem_limit_bytes=24 * MIB),
        cost_estimate=pl.CostEstimate(
            flops=8 * 10 ** 8 * (last - first), bytes_accessed=15 * 10 ** 6, transcendentals=0
        ),
        name="panel_columns",
    )(table, factors, turned)


def first_sum_kernel(at, table, *rest):
    ins, outs = rest[:2 * SIDE], rest[2 * SIDE:]
    for path, mine in enumerate((table[at.y], table[at.x])):
        for k in range(SIDE):
            to = lax.rem(mine + k, SIDE)
            total = ins[path * SIDE][to].astype(jnp.float32)
            for j in range(1, SIDE):
                total = total + ins[path * SIDE + j][to].astype(jnp.float32)
            out = outs[path * SIDE + k]
            out[...] = total.astype(out.dtype)


def first_sum(at, table, parts):
    shape = parts[0].shape[1:]
    return pl.pallas_call(
        functools.partial(first_sum_kernel, at),
        in_specs=[ON_SMEM] + [ON_VMEM] * len(parts),
        out_specs=[ON_VMEM] * len(parts),
        out_shape=[
            jax.ShapeDtypeStruct(shape, jnp.float32 if n % SIDE == 0 else jnp.bfloat16)
            for n in range(len(parts))
        ],
        compiler_params=pltpu.CompilerParams(vmem_limit_bytes=16 * MIB),
        name="first_sum",
    )(table, *parts)


def second_sum_kernel(skip, *refs):
    ins, own, mirrors = refs[:2 * SIDE], refs[2 * SIDE], refs[2 * SIDE + 1:]
    cut = ins[0].shape[0]
    size = 2 * cut
    for path in range(2):
        total = ins[path * SIDE][...]
        for j in range(1, SIDE):
            total = total + ins[path * SIDE + j][...].astype(jnp.float32)
        own[path * cut:(path + 1) * cut, :] = total
    for d, mirror in enumerate(mirrors, skip):
        mirror[...] = own[:, d * size:(d + 1) * size].T.astype(mirror.dtype)


def second_sum(skip, mirrors, parts):
    cut, span = parts[0].shape
    size = 2 * cut
    return pl.pallas_call(
        functools.partial(second_sum_kernel, skip),
        in_specs=[ON_VMEM] * len(parts),
        out_specs=[ON_VMEM] * (1 + mirrors),
        out_shape=[jax.ShapeDtypeStruct((size, span), jnp.float32)]
        + [jax.ShapeDtypeStruct((size, size), jnp.bfloat16)] * mirrors,
        compiler_params=pltpu.CompilerParams(vmem_limit_bytes=16 * MIB),
        name="second_sum",
    )(*parts)


def place_kernel(at, table, *rest):
    owns, mirrors, out = rest[:CHUNKS], rest[CHUNKS:-1], rest[-1]
    size = out.shape[0]
    ri = out.shape[1] // size
    d = 0
    for own in owns:
        for n in range(own.shape[1] // size):
            to = lax.rem(table[at.ri] + d, ri) * size
            out[:, pl.ds(pl.multiple_of(to, size), size)] = own[:, n * size:(n + 1) * size]
            d += 1
    for d, mirror in enumerate(mirrors, 1):
        to = lax.rem(table[at.ri] + ri - d, ri) * size
        out[:, pl.ds(pl.multiple_of(to, size), size)] = mirror[...].astype(out.dtype)


def place_blocks(at, table, owns, mirrors):
    size = owns[0].shape[0]
    ri = len(mirrors) * 2 + 2
    return pl.pallas_call(
        functools.partial(place_kernel, at),
        in_specs=[ON_SMEM] + [ON_VMEM] * (CHUNKS + len(mirrors)),
        out_specs=ON_VMEM,
        out_shape=jax.ShapeDtypeStruct((size, ri * size), jnp.float32),
        name="place_blocks",
    )(table, *owns, *mirrors)


def along_x(k):
    return [(y * SIDE + x, y * SIDE + (x + k) % SIDE) for y in range(SIDE) for x in range(SIDE)]


def along_y(k):
    return [(y * SIDE + x, (y + k) % SIDE * SIDE + x) for y in range(SIDE) for x in range(SIDE)]


def body(integrals, lam_index, tile_count, screen, coefficients, metric):
    ri = lax.axis_size("ri")
    at = Table(*integrals.shape[:2])
    here = lax.axis_index("ri").astype(jnp.int32)
    part = lax.axis_index("pair").astype(jnp.int32)
    place = jnp.stack([here, lax.rem(here, SIDE), lax.div(here, SIDE), lax.div(part, 2), lax.rem(part, 2)])
    table = prepare(at, place, lam_index, tile_count, screen)
    same, other = gather(coefficients)
    mine = fit(at, table, integrals, same, other)
    fitted = lax.all_to_all(mine, "ri", 0, 0, tiled=True)
    factors, turned = factor(metric, fitted)

    def exchange_two(parts, first, second):
        return (
            parts[:1] + [lax.ppermute(parts[k], "ri", first(k)) for k in range(1, SIDE)]
            + parts[SIDE:SIDE + 1] + [lax.ppermute(parts[SIDE + k], "ri", second(k)) for k in range(1, SIDE)]
        )

    cuts = (0, ri // 4 + 1, ri // 2 + 1)
    owns, mirrors = [], []
    for first, last in zip(cuts, cuts[1:]):
        skip = 1 if first == 0 else 0
        count = min(last, ri // 2) - first - skip
        panels = panel_columns(at, first, last, table, factors, turned)
        sums = first_sum(at, table, exchange_two(list(panels), along_x, along_y))
        own, *turned_blocks = second_sum(skip, count, exchange_two(list(sums), along_y, along_x))
        owns.append(own)
        for block in turned_blocks:
            d = len(mirrors) + 1
            mirrors.append(lax.ppermute(block, "ri", [(i, (i + d) % ri) for i in range(ri)]))
    return place_blocks(at, table, owns, mirrors)


def solution(mesh):
    placed = (
        P("pair", None, "ri", None, None),
        P("pair", None),
        P("pair"),
        P("pair", None),
        P(None, ("pair", "ri")),
        P(),
    )
    return jax.shard_map(
        body, mesh=mesh, in_specs=placed, out_specs=P(("pair", "ri"), None), check_vma=False
    )
```

```python
import functools

import jax
import jax.numpy as jnp
from jax import lax
from jax.experimental import pallas as pl
from jax.experimental.pallas import tpu as pltpu
from jax.sharding import PartitionSpec as P

MIB = 1024 * 1024
NT = (((1,), (1,)), ((), ()))
SIDE = 4
HALVES = 2
ON_VMEM = pl.BlockSpec(memory_space=pltpu.VMEM)
ON_SMEM = pl.BlockSpec(memory_space=pltpu.SMEM)
ANYWHERE = pl.BlockSpec(memory_space=pl.ANY)


class Chunk:
    def __init__(self, x_first, steps, hops, handed):
        self.x_first, self.steps, self.hops, self.handed = x_first, steps, hops, handed
        self.held = steps + [steps[n] for n, _ in hops]

    def arrivals(self):
        return [tuple(-d % SIDE for d in self.held[n]) for n in self.handed]


CHUNKS = (
    Chunk(False, [(0, 0), (1, 0), (1, 1), (1, 2), (1, 3)], [(2, 1), (3, 2), (4, 3)], [1, 5, 6, 7]),
    Chunk(True, [(0, 1), (0, 2), (2, 0), (2, 1), (2, 2)], [(3, 2)], [0, 5]),
)


class Table:
    def __init__(self, blocks, slots):
        self.blocks, self.slots = blocks, slots
        self.count = 0
        self.slot = self.count + blocks
        self.core = self.slot + blocks * slots
        self.top = self.core + blocks * slots
        self.low = self.top + blocks * slots
        self.ri = self.low + blocks * slots
        self.x, self.y = self.ri + 1, self.ri + 2
        self.size = self.ri + 3


def prepare_kernel(at, place, lam, tile_count, screen, table):
    ri, x, y, z, core = (place[n] for n in range(5))
    for n in range(3):
        table[at.ri + n] = place[n]

    def one(b, _):
        count = jnp.int32(0)
        for s in range(at.slots):
            name = lam[b, s]
            to = b * at.slots + count
            back_x = (x - name) & (SIDE - 1)
            back_y = (y - (name >> 2)) & (SIDE - 1)
            back_z = (z - (name >> 5)) & (SIDE - 1)
            table[at.slot + to] = s
            table[at.core + to] = ((name >> 4) ^ core) & 1
            table[at.top + to] = (back_y << 4) | (back_x << 2) | back_z
            table[at.low + to] = (back_x << 4) | (back_y << 2) | back_z
            keep = jnp.logical_and(s < tile_count[b], screen[b, s] > 0)
            count = count + keep.astype(jnp.int32)
        table[at.count + b] = count
        return 0

    lax.fori_loop(0, at.blocks, one, 0)


def prepare(at, place, lam, tile_count, screen):
    return pl.pallas_call(
        functools.partial(prepare_kernel, at),
        in_specs=[ON_SMEM] * 4,
        out_specs=ON_SMEM,
        out_shape=jax.ShapeDtypeStruct((at.size,), jnp.int32),
        name="prepare",
    )(place, lam, tile_count, screen)


def pack_kernel(count, *refs):
    ins, outs = refs[:-count], refs[-count:]
    each = len(ins) // count
    for n, out in enumerate(outs):
        for k in range(each):
            out[k] = ins[n * each + k][...]


def split_kernel(*refs):
    ins, (top, low) = refs[:-2], refs[-2:]
    half = top.shape[1]
    for k, part in enumerate(ins):
        top[k] = part[:half]
        low[k] = part[half:]


def cube_kernel(*refs):
    ins, out = refs[:-1], refs[-1]
    each = SIDE * SIDE
    for n, part in enumerate(ins):
        for k in range(SIDE):
            to = n % SIDE * each + k * SIDE
            out[n // SIDE, to:to + SIDE] = part[k]


def pack(kernel, shape, name, parts):
    return pl.pallas_call(
        kernel,
        in_specs=[ON_VMEM] * len(parts),
        out_specs=[ON_VMEM] * 2,
        out_shape=[jax.ShapeDtypeStruct((SIDE,) + shape, parts[0].dtype)] * 2,
        compiler_params=pltpu.CompilerParams(vmem_limit_bytes=16 * MIB),
        name=name,
    )(*parts)


def around(value, axis, shift):
    return [value] + [lax.ppermute(value, axis, shift(k)) for k in range(1, SIDE)]


def gather(coefficients):
    pairs = lax.axis_size("pair")
    size = coefficients.shape
    column = around(coefficients, "pair", lambda k: [(p, (p + 2 * k) % pairs) for p in range(pairs)])
    top, low = pack(split_kernel, (size[0] // 2, size[1]), "column", column)
    parts = around(top, "ri", along_x) + around(low, "ri", along_y)
    top, low = pack(functools.partial(pack_kernel, 2), top.shape, "plane", parts)
    parts = around(top, "ri", along_y) + around(low, "ri", along_x)
    same = pl.pallas_call(
        cube_kernel,
        in_specs=[ON_VMEM] * len(parts),
        out_specs=ON_VMEM,
        out_shape=jax.ShapeDtypeStruct((2, SIDE ** 3) + top.shape[2:], top.dtype),
        compiler_params=pltpu.CompilerParams(vmem_limit_bytes=16 * MIB),
        name="cube",
    )(*parts)
    return same, lax.ppermute(same, "pair", [(p, p ^ 1) for p in range(pairs)])


def fit_kernel(at, table, same, other, integrals, out, tiles, picked, total, done):
    slots = at.slots
    _, _, cut, size = same.shape
    ri, own_q, rows, _ = out.shape
    share = rows // HALVES
    steps = at.blocks // HALVES

    def copy(block, j):
        slot = table[at.slot + block * slots + j]
        return pltpu.make_async_copy(integrals.at[block, slot], tiles.at[block, j], done.at[block, j])

    def kept(block, act):
        for j in range(slots):
            @pl.when(j < table[at.count + block])
            def _():
                act(copy(block, j))

    def begin(step, _):
        for half in range(HALVES):
            kept(step + half * steps, lambda c: c.start())
        return 0

    lax.fori_loop(0, steps, begin, 0)

    def one(step, _):
        for half in range(HALVES):
            block = step + half * steps
            count = table[at.count + block]
            kept(block, lambda c: c.wait())

            @pl.when(count == 0)
            def _():
                total[half] = jnp.zeros(total.shape[1:], total.dtype)

            for c in range(1, slots + 1):
                @pl.when(count == c)
                def _():
                    for j in range(c):
                        n = block * slots + j
                        for part, start in enumerate((at.top, at.low)):
                            name = table[start + n]
                            tile = jnp.where(table[at.core + n] == 0, same[part, name], other[part, name])
                            picked[half, part * cut:(part + 1) * cut, j * size:(j + 1) * size] = tile
                    wide = [tiles[block, j].reshape(own_q * size, size) for j in range(c)]
                    wide = jnp.concatenate(wide, axis=1) if c > 1 else wide[0]
                    total[half] = lax.dot_general(
                        picked[half, :, :c * size], wide, NT, preferred_element_type=jnp.float32
                    )

        for q in range(own_q):
            parts = [
                total[half, :, q * size:(q + 1) * size].reshape(ri, share, size) for half in range(HALVES)
            ]
            out[:, q, :, pl.ds(pl.multiple_of(step * size, size), size)] = (
                jnp.concatenate(parts, axis=1).astype(out.dtype)
            )
        return 0

    lax.fori_loop(0, steps, one, 0)


def fit(at, table, integrals, same, other):
    blocks, slots, own_q, size, _ = integrals.shape
    occupied = 2 * same.shape[2]
    ri = SIDE * SIDE
    share = occupied // ri
    return pl.pallas_call(
        functools.partial(fit_kernel, at),
        in_specs=[ON_SMEM, ON_VMEM, ON_VMEM, ANYWHERE],
        out_specs=ON_VMEM,
        scratch_shapes=[
            pltpu.VMEM((blocks, slots, own_q, size, size), jnp.bfloat16),
            pltpu.VMEM((HALVES, occupied, slots * size), jnp.bfloat16),
            pltpu.VMEM((HALVES, occupied, own_q * size), jnp.float32),
            pltpu.SemaphoreType.DMA((blocks, slots)),
        ],
        out_shape=jax.ShapeDtypeStruct((ri, own_q, HALVES * share, blocks // HALVES * size), jnp.bfloat16),
        compiler_params=pltpu.CompilerParams(vmem_limit_bytes=40 * MIB),
        cost_estimate=pl.CostEstimate(flops=3 * 10 ** 9, bytes_accessed=20 * 10 ** 6, transcendentals=0),
        name="fit",
    )(table, same, other, integrals)


def factor_kernel(metric, fitted, factors, turned, wide):
    ri, own_q, rows, half_cols = fitted.shape
    share = rows // HALVES
    n_q = metric.shape[0]
    lanes, tile = wide.shape[1], wide.shape[3]
    chunk = lanes * tile

    def one(c, _):
        base = pl.multiple_of(c * chunk, chunk)
        for k in range(own_q):
            x = fitted[:, k, :, pl.ds(base, chunk)].astype(jnp.float32)
            for r in range(ri):
                to = (r * own_q + k) * share
                for h in range(HALVES):
                    for t in range(lanes):
                        wide[h, t, to:to + share, :] = x[r, h * share:(h + 1) * share, t * tile:(t + 1) * tile]
        for h in range(HALVES):
            start = pl.multiple_of(base + h * half_cols, chunk)
            parts = []
            for o in range(share):
                x = jnp.concatenate(
                    [wide[h, t, pl.ds(o, n_q, stride=share), :] for t in range(lanes)], axis=1
                ).astype(jnp.bfloat16)
                parts.append(jnp.dot(metric[...], x, preferred_element_type=jnp.float32).astype(jnp.bfloat16))
            whole = jnp.concatenate(parts, axis=0)
            factors[:, pl.ds(start, chunk)] = whole
            if h == 0:
                factors[:, pl.ds(pl.multiple_of(base + HALVES * half_cols, chunk), chunk)] = whole
            turned[pl.ds(start, chunk), :] = whole.T
        return 0

    lax.fori_loop(0, half_cols // chunk, one, 0)


def factor(metric, fitted):
    ri, own_q, rows, half_cols = fitted.shape
    cols = HALVES * half_cols
    depth = own_q * ri * rows // HALVES
    return pl.pallas_call(
        factor_kernel,
        in_specs=[ON_VMEM] * 2,
        out_specs=[ON_VMEM] * 2,
        out_shape=[
            jax.ShapeDtypeStruct((depth, cols + half_cols), jnp.bfloat16),
            jax.ShapeDtypeStruct((cols, depth), jnp.bfloat16),
        ],
        scratch_shapes=[pltpu.VMEM((HALVES, 2, depth, cols // ri), jnp.float32)],
        compiler_params=pltpu.CompilerParams(vmem_limit_bytes=28 * MIB),
        cost_estimate=pl.CostEstimate(flops=2 * 10 ** 9, bytes_accessed=10 * 10 ** 6, transcendentals=0),
        name="factor",
    )(metric, fitted)


def panel_kernel(at, chunk, table, factors, turned, *rest):
    outs, panels = rest[-1 - SIDE:-1], rest[-1]
    _, size, _ = panels.shape
    line = SIDE * size

    def row(y, _):
        for low in range(0, SIDE, 2):
            rows = turned[pl.ds(pl.multiple_of(y * line + low * size, 2 * size), 2 * size), :]
            for dy in sorted({dy for dy, _ in chunk.steps}):
                wanted = [dx for to, dx in chunk.steps if to == dy]
                first, last = (low, low + 2) if wanted == [0] else (0, SIDE)
                start = pl.multiple_of((y + dy) * line + first * size, 2 * size)
                value = jnp.dot(
                    rows, factors[:, pl.ds(start, (last - first) * size)], preferred_element_type=jnp.float32
                ).astype(jnp.bfloat16)
                for side in range(2):
                    x = low + side
                    for dx in wanted:
                        to = chunk.steps.index((dy, dx)) * size
                        at_col = ((x + dx) % SIDE - first) * size
                        panels[y * SIDE + x, :, to:to + size] = (
                            value[side * size:(side + 1) * size, at_col:at_col + size]
                        )
        return 0

    lax.fori_loop(0, SIDE, row, 0)
    for k in range(SIDE):
        to = lax.rem(table[at.x if chunk.x_first else at.y] + k, SIDE)
        for j in range(SIDE):
            outs[k][j] = panels[j * SIDE + to if chunk.x_first else to * SIDE + j]


def panel_columns(at, chunk, weight, table, factors, turned, *after):
    cols, depth = turned.shape
    size = cols // (SIDE * SIDE)
    span = len(chunk.steps) * size
    return pl.pallas_call(
        functools.partial(panel_kernel, at, chunk),
        in_specs=[ON_SMEM, ON_VMEM, ON_VMEM] + [ANYWHERE] * len(after),
        out_specs=[ON_VMEM] * SIDE,
        out_shape=[jax.ShapeDtypeStruct((SIDE, size, span), jnp.bfloat16)] * SIDE,
        scratch_shapes=[pltpu.VMEM((SIDE * SIDE, size, span), jnp.bfloat16)],
        compiler_params=pltpu.CompilerParams(vmem_limit_bytes=24 * MIB),
        cost_estimate=pl.CostEstimate(
            flops=weight * 4 * 10 ** 9, bytes_accessed=15 * 10 ** 6, transcendentals=0
        ),
        name="panel_columns",
    )(table, factors, turned, *after)


def first_sum_kernel(at, chunk, table, *rest):
    ins, outs = rest[:SIDE], rest[SIDE:]
    size = ins[0].shape[1]
    own = len(chunk.steps) * size
    mine = table[at.y if chunk.x_first else at.x]

    def total(panel, start, stop):
        value = ins[0][panel, :, start:stop].astype(jnp.float32)
        for part in ins[1:]:
            value = value + part[panel, :, start:stop].astype(jnp.float32)
        return value

    for k, out in enumerate(outs):
        to = mine + k
        out[:, :own] = total(lax.rem(to, SIDE), 0, own).astype(out.dtype)
        for n, (position, back) in enumerate(chunk.hops):
            start = position * size
            value = total(lax.rem(to + SIDE - back, SIDE), start, start + size)
            out[:, own + n * size:own + (n + 1) * size] = value.astype(out.dtype)


def first_sum(at, chunk, table, parts):
    size = parts[0].shape[1]
    shape = (size, len(chunk.held) * size)
    return pl.pallas_call(
        functools.partial(first_sum_kernel, at, chunk),
        in_specs=[ON_SMEM] + [ON_VMEM] * SIDE,
        out_specs=[ON_VMEM] * SIDE,
        out_shape=[jax.ShapeDtypeStruct(shape, jnp.bfloat16 if n else jnp.float32) for n in range(SIDE)],
        compiler_params=pltpu.CompilerParams(vmem_limit_bytes=16 * MIB),
        name="first_sum",
    )(table, *parts)


def second_sum_kernel(chunk, *refs):
    ins, own, handed = refs[:SIDE], refs[SIDE], refs[SIDE + 1]
    size, span = own.shape
    for n in range(len(chunk.held)):
        total = ins[0][:, n * size:(n + 1) * size]
        for part in ins[1:]:
            total = total + part[:, n * size:(n + 1) * size].astype(jnp.float32)
        if n * size < span:
            own[:, n * size:(n + 1) * size] = total
        if n in chunk.handed:
            handed[chunk.handed.index(n)] = total.T.astype(handed.dtype)


def second_sum(chunk, parts):
    size = parts[0].shape[0]
    return pl.pallas_call(
        functools.partial(second_sum_kernel, chunk),
        in_specs=[ON_VMEM] * SIDE,
        out_specs=[ON_VMEM] * 2,
        out_shape=[
            jax.ShapeDtypeStruct((size, len(chunk.steps) * size), jnp.float32),
            jax.ShapeDtypeStruct((len(chunk.handed), size, size), jnp.bfloat16),
        ],
        compiler_params=pltpu.CompilerParams(vmem_limit_bytes=16 * MIB),
        name="second_sum",
    )(*parts)


def place_kernel(at, table, *rest):
    owns, mirrors, out = rest[:len(CHUNKS)], rest[len(CHUNKS):-1], rest[-1]
    size = out.shape[0]

    def put(step, value):
        y = lax.rem(table[at.y] + step[0], SIDE)
        x = lax.rem(table[at.x] + step[1], SIDE)
        out[:, pl.ds(pl.multiple_of((y * SIDE + x) * size, size), size)] = value.astype(out.dtype)

    for chunk, own, mirror in zip(CHUNKS, owns, mirrors):
        for n, step in enumerate(chunk.steps):
            put(step, own[:, n * size:(n + 1) * size])
        for n, step in enumerate(chunk.arrivals()):
            put(step, mirror[n])


def place_blocks(at, table, owns, mirrors):
    size = owns[0].shape[0]
    return pl.pallas_call(
        functools.partial(place_kernel, at),
        in_specs=[ON_SMEM] + [ON_VMEM] * (len(owns) + len(mirrors)),
        out_specs=ON_VMEM,
        out_shape=jax.ShapeDtypeStruct((size, SIDE * SIDE * size), jnp.float32),
        compiler_params=pltpu.CompilerParams(vmem_limit_bytes=16 * MIB),
        name="place_blocks",
    )(table, *owns, *mirrors)


def along_x(k):
    return [(y * SIDE + x, y * SIDE + (x + k) % SIDE) for y in range(SIDE) for x in range(SIDE)]


def along_y(k):
    return [(y * SIDE + x, (y + k) % SIDE * SIDE + x) for y in range(SIDE) for x in range(SIDE)]


def body(integrals, lam_index, tile_count, screen, coefficients, metric):
    ri = lax.axis_size("ri")
    at = Table(*integrals.shape[:2])
    here = lax.axis_index("ri").astype(jnp.int32)
    part = lax.axis_index("pair").astype(jnp.int32)
    place = jnp.stack([here, lax.rem(here, SIDE), lax.div(here, SIDE), lax.div(part, 2), lax.rem(part, 2)])
    table = prepare(at, place, lam_index, tile_count, screen)
    same, other = gather(coefficients)
    mine = fit(at, table, integrals, same, other)
    fitted = lax.all_to_all(mine, "ri", 0, 0, tiled=True)
    factors, turned = factor(metric, fitted)

    def send(parts, way):
        return [parts[0]] + [lax.ppermute(parts[k], "ri", way(k)) for k in range(1, SIDE)]

    owns, mirrors, after = [], [], []
    for chunk in CHUNKS:
        ways = (along_x, along_y) if chunk.x_first else (along_y, along_x)
        panels = panel_columns(at, chunk, 20 if after else 1, table, factors, turned, *after)
        after = [panels[0]]
        sums = first_sum(at, chunk, table, send(panels, ways[0]))
        own, handed = second_sum(chunk, send(sums, ways[1]))
        owns.append(own)
        mirrors.append(lax.ppermute(handed, "ri", ways[0](1)))
    return place_blocks(at, table, owns, mirrors)


def solution(mesh):
    placed = (
        P("pair", None, "ri", None, None),
        P("pair", None),
        P("pair"),
        P("pair", None),
        P(None, ("pair", "ri")),
        P(),
    )
    return jax.shard_map(
        body, mesh=mesh, in_specs=placed, out_specs=P(("pair", "ri"), None), check_vma=False
    )
```

```python
import functools

import jax
import jax.numpy as jnp
from jax import lax
from jax.experimental import pallas as pl
from jax.experimental.pallas import tpu as pltpu
from jax.sharding import PartitionSpec as P

MIB = 1024 * 1024
NT = (((1,), (1,)), ((), ()))
SIDE = 4
HALVES = 2
ON_VMEM = pl.BlockSpec(memory_space=pltpu.VMEM)
ON_SMEM = pl.BlockSpec(memory_space=pltpu.SMEM)
ANYWHERE = pl.BlockSpec(memory_space=pl.ANY)


class Chunk:
    def __init__(self, x_first, steps, hops, handed):
        self.x_first, self.steps, self.hops, self.handed = x_first, steps, hops, handed
        self.held = steps + [steps[n] for n, _ in hops]

    def arrivals(self):
        return [tuple(-d % SIDE for d in self.held[n]) for n in self.handed]


CHUNKS = (
    Chunk(False, [(0, 0), (1, 0), (1, 1), (1, 2), (1, 3)], [(2, 1), (3, 2), (4, 3)], [1, 5, 6, 7]),
    Chunk(True, [(0, 1), (0, 2), (2, 0), (2, 1), (2, 2)], [(3, 2)], [0, 5]),
)


class Table:
    def __init__(self, blocks, slots):
        self.blocks, self.slots = blocks, slots
        self.count = 0
        self.slot = self.count + blocks
        self.core = self.slot + blocks * slots
        self.name = self.core + blocks * slots
        self.x = self.name + blocks * slots
        self.y = self.x + 1
        self.size = self.y + 1


def prepare_kernel(at, place, lam, tile_count, screen, table):
    core = place[0]
    table[at.x] = place[1]
    table[at.y] = place[2]

    def one(b, _):
        count = jnp.int32(0)
        for s in range(at.slots):
            name = lam[b, s]
            to = b * at.slots + count
            table[at.slot + to] = s
            table[at.core + to] = ((name >> 4) ^ core) & 1
            table[at.name + to] = ((name >> 5) << 4) | (name & 15)
            keep = jnp.logical_and(s < tile_count[b], screen[b, s] > 0)
            count = count + keep.astype(jnp.int32)
        table[at.count + b] = count
        return 0

    lax.fori_loop(0, at.blocks, one, 0)


def prepare(at, place, lam, tile_count, screen):
    return pl.pallas_call(
        functools.partial(prepare_kernel, at),
        in_specs=[ON_SMEM] * 4,
        out_specs=ON_SMEM,
        out_shape=jax.ShapeDtypeStruct((at.size,), jnp.int32),
        name="prepare",
    )(place, lam, tile_count, screen)


def gather(coefficients):
    copies = jnp.broadcast_to(coefficients[None], (lax.axis_size(("z", "y", "x")),) + coefficients.shape)
    same = lax.all_to_all(copies, ("z", "y", "x"), 0, 0, tiled=True)
    return same, lax.ppermute(same, "core", [(0, 1), (1, 0)])


def fit_kernel(at, table, same, other, integrals, out, tiles, picked, total, done):
    slots = at.slots
    _, _, size = same.shape
    ri, own_q, rows, _ = out.shape
    share = rows // HALVES
    steps = at.blocks // HALVES

    def copy(block, j):
        slot = table[at.slot + block * slots + j]
        return pltpu.make_async_copy(integrals.at[block, slot], tiles.at[block, j], done.at[block, j])

    def kept(block, act):
        for j in range(slots):
            @pl.when(j < table[at.count + block])
            def _():
                act(copy(block, j))

    def begin(step, _):
        for half in range(HALVES):
            kept(step + half * steps, lambda c: c.start())
        return 0

    lax.fori_loop(0, steps, begin, 0)

    def one(step, _):
        for half in range(HALVES):
            block = step + half * steps
            count = table[at.count + block]
            kept(block, lambda c: c.wait())

            @pl.when(count == 0)
            def _():
                total[half] = jnp.zeros(total.shape[1:], total.dtype)

            for c in range(1, slots + 1):
                @pl.when(count == c)
                def _():
                    for j in range(c):
                        n = block * slots + j
                        name = table[at.name + n]
                        tile = jnp.where(table[at.core + n] == 0, same[name], other[name])
                        picked[half, :, j * size:(j + 1) * size] = tile
                    wide = [tiles[block, j].reshape(own_q * size, size) for j in range(c)]
                    wide = jnp.concatenate(wide, axis=1) if c > 1 else wide[0]
                    total[half] = lax.dot_general(
                        picked[half, :, :c * size], wide, NT, preferred_element_type=jnp.float32
                    )

        for q in range(own_q):
            parts = [
                total[half, :, q * size:(q + 1) * size].reshape(ri, share, size) for half in range(HALVES)
            ]
            out[:, q, :, pl.ds(pl.multiple_of(step * size, size), size)] = (
                jnp.concatenate(parts, axis=1).astype(out.dtype)
            )
        return 0

    lax.fori_loop(0, steps, one, 0)


def fit(at, table, integrals, same, other):
    blocks, slots, own_q, size, _ = integrals.shape
    occupied = same.shape[1]
    ri = SIDE * SIDE
    share = occupied // ri
    return pl.pallas_call(
        functools.partial(fit_kernel, at),
        in_specs=[ON_SMEM, ON_VMEM, ON_VMEM, ANYWHERE],
        out_specs=ON_VMEM,
        scratch_shapes=[
            pltpu.VMEM((blocks, slots, own_q, size, size), jnp.bfloat16),
            pltpu.VMEM((HALVES, occupied, slots * size), jnp.bfloat16),
            pltpu.VMEM((HALVES, occupied, own_q * size), jnp.float32),
            pltpu.SemaphoreType.DMA((blocks, slots)),
        ],
        out_shape=jax.ShapeDtypeStruct((ri, own_q, HALVES * share, blocks // HALVES * size), jnp.bfloat16),
        compiler_params=pltpu.CompilerParams(vmem_limit_bytes=40 * MIB),
        cost_estimate=pl.CostEstimate(flops=3 * 10 ** 9, bytes_accessed=20 * 10 ** 6, transcendentals=0),
        name="fit",
    )(table, same, other, integrals)


def factor_kernel(metric, fitted, factors, turned, wide):
    ri, own_q, rows, half_cols = fitted.shape
    share = rows // HALVES
    n_q = metric.shape[0]
    lanes, tile = wide.shape[1], wide.shape[3]
    chunk = lanes * tile

    def one(c, _):
        base = pl.multiple_of(c * chunk, chunk)
        for k in range(own_q):
            x = fitted[:, k, :, pl.ds(base, chunk)].astype(jnp.float32)
            for r in range(ri):
                to = (r * own_q + k) * share
                for h in range(HALVES):
                    for t in range(lanes):
                        wide[h, t, to:to + share, :] = x[r, h * share:(h + 1) * share, t * tile:(t + 1) * tile]
        for h in range(HALVES):
            start = pl.multiple_of(base + h * half_cols, chunk)
            parts = []
            for o in range(share):
                x = jnp.concatenate(
                    [wide[h, t, pl.ds(o, n_q, stride=share), :] for t in range(lanes)], axis=1
                ).astype(jnp.bfloat16)
                parts.append(jnp.dot(metric[...], x, preferred_element_type=jnp.float32).astype(jnp.bfloat16))
            whole = jnp.concatenate(parts, axis=0)
            factors[:, pl.ds(start, chunk)] = whole
            turned[pl.ds(start, chunk), :] = whole.T
        return 0

    lax.fori_loop(0, half_cols // chunk, one, 0)


def factor(metric, fitted):
    ri, own_q, rows, half_cols = fitted.shape
    cols = HALVES * half_cols
    depth = own_q * ri * rows // HALVES
    return pl.pallas_call(
        factor_kernel,
        in_specs=[ON_VMEM] * 2,
        out_specs=[ON_VMEM] * 2,
        out_shape=[
            jax.ShapeDtypeStruct((depth, cols), jnp.bfloat16),
            jax.ShapeDtypeStruct((cols, depth), jnp.bfloat16),
        ],
        scratch_shapes=[pltpu.VMEM((HALVES, 2, depth, cols // ri), jnp.float32)],
        compiler_params=pltpu.CompilerParams(vmem_limit_bytes=20 * MIB),
        cost_estimate=pl.CostEstimate(flops=2 * 10 ** 9, bytes_accessed=10 * 10 ** 6, transcendentals=0),
        name="factor",
    )(metric, fitted)


def panel_kernel(at, chunk, table, factors, turned, *rest):
    outs, panels = rest[-1 - SIDE:-1], rest[-1]
    _, size, _ = panels.shape
    line = SIDE * size

    def row(y, _):
        for dy in sorted({dy for dy, _ in chunk.steps}):
            wanted = [dx for to, dx in chunk.steps if to == dy]
            side = 2 if wanted == [0] else SIDE
            for low in range(0, SIDE, side):
                rows = turned[pl.ds(pl.multiple_of(y * line + low * size, side * size), side * size), :]
                start = pl.multiple_of(lax.rem(y + dy, SIDE) * line + low * size, side * size)
                value = jnp.dot(
                    rows, factors[:, pl.ds(start, side * size)], preferred_element_type=jnp.float32
                ).astype(jnp.bfloat16)
                for n in range(side):
                    for dx in wanted:
                        to = chunk.steps.index((dy, dx)) * size
                        col = (n + dx) % side * size
                        x = low + n
                        panels[y * SIDE + x, :, to:to + size] = value[n * size:(n + 1) * size, col:col + size]
        return 0

    lax.fori_loop(0, SIDE, row, 0)
    for k, out in enumerate(outs):
        to = lax.rem(table[at.x if chunk.x_first else at.y] + k, SIDE)
        for j in range(SIDE):
            out[j] = panels[j * SIDE + to if chunk.x_first else to * SIDE + j]


def panel_columns(at, chunk, weight, table, factors, turned, *after):
    cols, depth = turned.shape
    size = cols // (SIDE * SIDE)
    span = len(chunk.steps) * size
    return pl.pallas_call(
        functools.partial(panel_kernel, at, chunk),
        in_specs=[ON_SMEM, ON_VMEM, ON_VMEM] + [ANYWHERE] * len(after),
        out_specs=[ON_VMEM] * SIDE,
        out_shape=[jax.ShapeDtypeStruct((SIDE, size, span), jnp.bfloat16)] * SIDE,
        scratch_shapes=[pltpu.VMEM((SIDE * SIDE, size, span), jnp.bfloat16)],
        compiler_params=pltpu.CompilerParams(vmem_limit_bytes=12 * MIB),
        cost_estimate=pl.CostEstimate(
            flops=weight * 4 * 10 ** 9, bytes_accessed=15 * 10 ** 6, transcendentals=0
        ),
        name="panel_columns",
    )(table, factors, turned, *after)


def first_sum_kernel(at, chunk, table, *rest):
    ins, outs = rest[:SIDE], rest[-SIDE:]
    size = outs[0].shape[0]
    own = len(chunk.steps) * size
    mine = table[at.y if chunk.x_first else at.x]

    def total(panel, start, stop):
        value = ins[0][panel, :, start:stop].astype(jnp.float32)
        for part in ins[1:]:
            value = value + part[panel, :, start:stop].astype(jnp.float32)
        return value

    for k, out in enumerate(outs):
        to = mine + k
        out[:, :own] = total(lax.rem(to, SIDE), 0, own).astype(out.dtype)
        for n, (position, back) in enumerate(chunk.hops):
            start = position * size
            value = total(lax.rem(to + SIDE - back, SIDE), start, start + size)
            out[:, own + n * size:own + (n + 1) * size] = value.astype(out.dtype)


def first_sum(at, chunk, table, parts):
    size = parts[0].shape[-2]
    shape = (size, len(chunk.held) * size)
    return pl.pallas_call(
        functools.partial(first_sum_kernel, at, chunk),
        in_specs=[ON_SMEM] + [ON_VMEM] * SIDE,
        out_specs=[ON_VMEM] * SIDE,
        out_shape=[jax.ShapeDtypeStruct(shape, jnp.bfloat16 if n else jnp.float32) for n in range(SIDE)],
        compiler_params=pltpu.CompilerParams(vmem_limit_bytes=16 * MIB),
        name="first_sum",
    )(table, *parts)


def second_sum_kernel(chunk, *refs):
    parts, own, handed = refs[:SIDE], refs[SIDE], refs[SIDE + 1]
    size, span = own.shape
    for n in range(len(chunk.held)):
        total = parts[0][:, n * size:(n + 1) * size]
        for part in parts[1:]:
            total = total + part[:, n * size:(n + 1) * size].astype(jnp.float32)
        if n * size < span:
            own[:, n * size:(n + 1) * size] = total
        if n in chunk.handed:
            handed[chunk.handed.index(n)] = total.T.astype(handed.dtype)


def second_sum(chunk, parts):
    size = parts[0].shape[0]
    return pl.pallas_call(
        functools.partial(second_sum_kernel, chunk),
        in_specs=[ON_VMEM] * SIDE,
        out_specs=[ON_VMEM] * 2,
        out_shape=[
            jax.ShapeDtypeStruct((size, len(chunk.steps) * size), jnp.float32),
            jax.ShapeDtypeStruct((len(chunk.handed), size, size), jnp.bfloat16),
        ],
        compiler_params=pltpu.CompilerParams(vmem_limit_bytes=16 * MIB),
        name="second_sum",
    )(*parts)


def place_kernel(at, table, *rest):
    owns, mirrors, out = rest[:len(CHUNKS)], rest[len(CHUNKS):-1], rest[-1]
    size = out.shape[0]

    def put(step, value):
        y = lax.rem(table[at.y] + step[0], SIDE)
        x = lax.rem(table[at.x] + step[1], SIDE)
        out[:, pl.ds(pl.multiple_of((y * SIDE + x) * size, size), size)] = value.astype(out.dtype)

    for chunk, own, mirror in zip(CHUNKS, owns, mirrors):
        for n, step in enumerate(chunk.steps):
            put(step, own[:, n * size:(n + 1) * size])
        for n, step in enumerate(chunk.arrivals()):
            put(step, mirror[n])


def place_blocks(at, table, owns, mirrors):
    size = owns[0].shape[0]
    return pl.pallas_call(
        functools.partial(place_kernel, at),
        in_specs=[ON_SMEM] + [ON_VMEM] * (len(owns) + len(mirrors)),
        out_specs=ON_VMEM,
        out_shape=jax.ShapeDtypeStruct((size, SIDE * SIDE * size), jnp.float32),
        compiler_params=pltpu.CompilerParams(vmem_limit_bytes=16 * MIB),
        name="place_blocks",
    )(table, *owns, *mirrors)


def along(axis, k):
    return functools.partial(lax.ppermute, axis_name=axis, perm=[(i, (i + k) % SIDE) for i in range(SIDE)])


def body(integrals, lam_index, tile_count, screen, coefficients, metric):
    at = Table(*integrals.shape[:2])
    place = jnp.stack([lax.axis_index(name).astype(jnp.int32) for name in ("core", "x", "y")])
    table = prepare(at, place, lam_index, tile_count, screen)
    same, other = gather(coefficients)
    mine = fit(at, table, integrals, same, other)
    fitted = lax.all_to_all(mine, ("y", "x"), 0, 0, tiled=True)
    factors, turned = factor(metric, fitted)

    def send(parts, axis):
        return [parts[0]] + [along(axis, k)(parts[k]) for k in range(1, SIDE)]

    owns, mirrors, after = [], [], []
    for chunk in CHUNKS:
        first, second = ("x", "y") if chunk.x_first else ("y", "x")
        panels = panel_columns(at, chunk, 20 if after else 1, table, factors, turned, *after)
        after = [panels[0]]
        sums = first_sum(at, chunk, table, send(panels, first))
        own, handed = second_sum(chunk, send(sums, second))
        owns.append(own)
        mirrors.append(along(first, 1)(handed))
    return place_blocks(at, table, owns, mirrors)


def solution(mesh):
    pair, ri = ("z", "core"), ("y", "x")
    cores = 2
    devices = mesh.devices.reshape(mesh.shape["pair"] // cores, cores, SIDE, SIDE)
    named = jax.sharding.Mesh(devices, pair + ri)
    placed = (
        P(pair, None, ri, None, None),
        P(pair, None),
        P(pair),
        P(pair, None),
        P(None, pair + ri),
        P(),
    )
    return jax.shard_map(
        body, mesh=named, in_specs=placed, out_specs=P(pair + ri, None), check_vma=False
    )
```

```python
import functools

import jax
import jax.numpy as jnp
from jax import lax
from jax.experimental import pallas as pl
from jax.experimental.pallas import tpu as pltpu
from jax.sharding import PartitionSpec as P

MIB = 1024 * 1024
NT = (((1,), (1,)), ((), ()))
SIDE = 4
HALVES = 2
ON_VMEM = pl.BlockSpec(memory_space=pltpu.VMEM)
ON_SMEM = pl.BlockSpec(memory_space=pltpu.SMEM)
ANYWHERE = pl.BlockSpec(memory_space=pl.ANY)


class Chunk:
    def __init__(self, x_first, steps, hops, handed):
        self.x_first, self.steps, self.hops, self.handed = x_first, steps, hops, handed
        self.held = steps + [steps[n] for n, _ in hops]

    def arrivals(self):
        return [tuple(-d % SIDE for d in self.held[n]) for n in self.handed]


CHUNKS = (
    Chunk(False, [(0, 0), (1, 0), (1, 1), (1, 2), (1, 3)], [(2, 1), (3, 2), (4, 3)], [1, 5, 6, 7]),
    Chunk(True, [(0, 1), (0, 2), (2, 0), (2, 1), (2, 2)], [(3, 2)], [0, 5]),
)


class Table:
    def __init__(self, blocks, slots):
        self.blocks, self.slots = blocks, slots
        self.count = 0
        self.slot = self.count + blocks
        self.core = self.slot + blocks * slots
        self.name = self.core + blocks * slots
        self.x = self.name + blocks * slots
        self.y = self.x + 1
        self.size = self.y + 1


def prepare_kernel(at, place, lam, tile_count, screen, table):
    core = place[0]
    table[at.x] = place[1]
    table[at.y] = place[2]

    def one(b, _):
        count = jnp.int32(0)
        for s in range(at.slots):
            name = lam[b, s]
            to = b * at.slots + count
            table[at.slot + to] = s
            table[at.core + to] = ((name >> 4) ^ core) & 1
            table[at.name + to] = ((name >> 5) << 4) | (name & 15)
            keep = jnp.logical_and(s < tile_count[b], screen[b, s] > 0)
            count = count + keep.astype(jnp.int32)
        table[at.count + b] = count
        return 0

    lax.fori_loop(0, at.blocks, one, 0)


def prepare(at, place, lam, tile_count, screen):
    return pl.pallas_call(
        functools.partial(prepare_kernel, at),
        in_specs=[ON_SMEM] * 4,
        out_specs=ON_SMEM,
        out_shape=jax.ShapeDtypeStruct((at.size,), jnp.int32),
        name="prepare",
    )(place, lam, tile_count, screen)


def gather(coefficients):
    copies = jnp.broadcast_to(coefficients[None], (lax.axis_size(("z", "y", "x")),) + coefficients.shape)
    same = lax.all_to_all(copies, ("z", "y", "x"), 0, 0, tiled=True)
    return same, lax.ppermute(same, "core", [(0, 1), (1, 0)])


def fit_kernel(at, table, same, other, integrals, out, tiles, picked, total, done):
    slots = at.slots
    _, _, size = same.shape
    ri, own_q, rows, _ = out.shape
    share = rows // HALVES
    steps = at.blocks // HALVES

    def copy(block, j):
        slot = table[at.slot + block * slots + j]
        return pltpu.make_async_copy(integrals.at[block, slot], tiles.at[block, j], done.at[block, j])

    def kept(block, act):
        for j in range(slots):
            @pl.when(j < table[at.count + block])
            def _():
                act(copy(block, j))

    def begin(step, _):
        for half in range(HALVES):
            kept(step + half * steps, lambda c: c.start())
        return 0

    lax.fori_loop(0, steps, begin, 0)

    def one(step, _):
        for half in range(HALVES):
            block = step + half * steps
            count = table[at.count + block]
            kept(block, lambda c: c.wait())

            @pl.when(count == 0)
            def _():
                total[half] = jnp.zeros(total.shape[1:], total.dtype)

            for c in range(1, slots + 1):
                @pl.when(count == c)
                def _():
                    for j in range(c):
                        n = block * slots + j
                        name = table[at.name + n]
                        tile = jnp.where(table[at.core + n] == 0, same[name], other[name])
                        picked[half, :, j * size:(j + 1) * size] = tile
                    wide = [tiles[block, j].reshape(own_q * size, size) for j in range(c)]
                    wide = jnp.concatenate(wide, axis=1) if c > 1 else wide[0]
                    total[half] = lax.dot_general(
                        picked[half, :, :c * size], wide, NT, preferred_element_type=jnp.float32
                    )

        for q in range(own_q):
            parts = [
                total[half, :, q * size:(q + 1) * size].reshape(ri, share, size) for half in range(HALVES)
            ]
            out[:, q, :, pl.ds(pl.multiple_of(step * size, size), size)] = (
                jnp.concatenate(parts, axis=1).astype(out.dtype)
            )
        return 0

    lax.fori_loop(0, steps, one, 0)


def fit(at, table, integrals, same, other):
    blocks, slots, own_q, size, _ = integrals.shape
    occupied = same.shape[1]
    ri = SIDE * SIDE
    share = occupied // ri
    return pl.pallas_call(
        functools.partial(fit_kernel, at),
        in_specs=[ON_SMEM, ON_VMEM, ON_VMEM, ANYWHERE],
        out_specs=ON_VMEM,
        scratch_shapes=[
            pltpu.VMEM((blocks, slots, own_q, size, size), jnp.bfloat16),
            pltpu.VMEM((HALVES, occupied, slots * size), jnp.bfloat16),
            pltpu.VMEM((HALVES, occupied, own_q * size), jnp.float32),
            pltpu.SemaphoreType.DMA((blocks, slots)),
        ],
        out_shape=jax.ShapeDtypeStruct((ri, own_q, HALVES * share, blocks // HALVES * size), jnp.bfloat16),
        compiler_params=pltpu.CompilerParams(vmem_limit_bytes=40 * MIB),
        cost_estimate=pl.CostEstimate(flops=3 * 10 ** 9, bytes_accessed=20 * 10 ** 6, transcendentals=0),
        name="fit",
    )(table, same, other, integrals)


def factor_kernel(metric, fitted, factors, turned, wide):
    ri, own_q, rows, half_cols = fitted.shape
    share = rows // HALVES
    n_q = metric.shape[0]
    lanes, tile = wide.shape[1], wide.shape[3]
    chunk = lanes * tile

    def one(c, _):
        base = pl.multiple_of(c * chunk, chunk)
        for k in range(own_q):
            x = fitted[:, k, :, pl.ds(base, chunk)].astype(jnp.float32)
            for r in range(ri):
                to = (r * own_q + k) * share
                for h in range(HALVES):
                    for t in range(lanes):
                        wide[h, t, to:to + share, :] = x[r, h * share:(h + 1) * share, t * tile:(t + 1) * tile]
        for h in range(HALVES):
            start = pl.multiple_of(base + h * half_cols, chunk)
            parts = []
            for o in range(share):
                x = jnp.concatenate(
                    [wide[h, t, pl.ds(o, n_q, stride=share), :] for t in range(lanes)], axis=1
                ).astype(jnp.bfloat16)
                parts.append(jnp.dot(metric[...], x, preferred_element_type=jnp.float32).astype(jnp.bfloat16))
            whole = jnp.concatenate(parts, axis=0)
            factors[:, pl.ds(start, chunk)] = whole
            turned[pl.ds(start, chunk), :] = whole.T
        return 0

    lax.fori_loop(0, half_cols // chunk, one, 0)


def factor(metric, fitted):
    ri, own_q, rows, half_cols = fitted.shape
    cols = HALVES * half_cols
    depth = own_q * ri * rows // HALVES
    return pl.pallas_call(
        factor_kernel,
        in_specs=[ON_VMEM] * 2,
        out_specs=[ON_VMEM] * 2,
        out_shape=[
            jax.ShapeDtypeStruct((depth, cols), jnp.bfloat16),
            jax.ShapeDtypeStruct((cols, depth), jnp.bfloat16),
        ],
        scratch_shapes=[pltpu.VMEM((HALVES, 2, depth, cols // ri), jnp.float32)],
        compiler_params=pltpu.CompilerParams(vmem_limit_bytes=20 * MIB),
        cost_estimate=pl.CostEstimate(flops=2 * 10 ** 9, bytes_accessed=10 * 10 ** 6, transcendentals=0),
        name="factor",
    )(metric, fitted)


def panel_kernel(at, table, factors, turned, *rest):
    outs, panels = rest[:-1], rest[-1]
    size = panels.shape[1]
    line = SIDE * size
    for k in range(SIDE):
        y = lax.rem(table[at.y] + k, SIDE)
        rows = turned[pl.ds(pl.multiple_of(y * line, line), line), :]
        for dy in sorted({dy for chunk in CHUNKS for dy, _ in chunk.steps}):
            start = pl.multiple_of(lax.rem(y + dy, SIDE) * line, line)
            value = jnp.dot(
                rows, factors[:, pl.ds(start, line)], preferred_element_type=jnp.float32
            ).astype(jnp.bfloat16)
            for n, chunk in enumerate(CHUNKS):
                for position, step in enumerate(chunk.steps):
                    if step[0] != dy:
                        continue
                    to = position * size
                    for x in range(SIDE):
                        col = (x + step[1]) % SIDE * size
                        block = value[x * size:(x + 1) * size, col:col + size]
                        if chunk.x_first:
                            panels[y * SIDE + x, :, to:to + size] = block
                        else:
                            outs[n * SIDE + k][x, :, to:to + size] = block
    for n, chunk in enumerate(CHUNKS):
        if chunk.x_first:
            for k in range(SIDE):
                x = lax.rem(table[at.x] + k, SIDE)
                for y in range(SIDE):
                    outs[n * SIDE + k][y] = panels[y * SIDE + x]


def panel_columns(at, table, factors, turned):
    cols, depth = turned.shape
    size = cols // (SIDE * SIDE)
    widest = max(len(chunk.steps) for chunk in CHUNKS if chunk.x_first) * size
    return pl.pallas_call(
        functools.partial(panel_kernel, at),
        in_specs=[ON_SMEM, ON_VMEM, ON_VMEM],
        out_specs=[ON_VMEM] * (len(CHUNKS) * SIDE),
        out_shape=[
            jax.ShapeDtypeStruct((SIDE, size, len(chunk.steps) * size), jnp.bfloat16)
            for chunk in CHUNKS
            for _ in range(SIDE)
        ],
        scratch_shapes=[pltpu.VMEM((SIDE * SIDE, size, widest), jnp.bfloat16)],
        compiler_params=pltpu.CompilerParams(vmem_limit_bytes=16 * MIB),
        cost_estimate=pl.CostEstimate(flops=8 * 10 ** 9, bytes_accessed=15 * 10 ** 6, transcendentals=0),
        name="panel_columns",
    )(table, factors, turned)


def first_sum_kernel(at, chunk, table, *rest):
    ins, outs = rest[:SIDE], rest[-SIDE:]
    size = outs[0].shape[0]
    own = len(chunk.steps) * size
    mine = table[at.y if chunk.x_first else at.x]

    def total(panel, start, stop):
        value = ins[0][panel, :, start:stop].astype(jnp.float32)
        for part in ins[1:]:
            value = value + part[panel, :, start:stop].astype(jnp.float32)
        return value

    for k, out in enumerate(outs):
        to = mine + k
        out[:, :own] = total(lax.rem(to, SIDE), 0, own).astype(out.dtype)
        for n, (position, back) in enumerate(chunk.hops):
            start = position * size
            value = total(lax.rem(to + SIDE - back, SIDE), start, start + size)
            out[:, own + n * size:own + (n + 1) * size] = value.astype(out.dtype)


def first_sum(at, chunk, table, parts):
    size = parts[0].shape[-2]
    shape = (size, len(chunk.held) * size)
    return pl.pallas_call(
        functools.partial(first_sum_kernel, at, chunk),
        in_specs=[ON_SMEM] + [ON_VMEM] * SIDE,
        out_specs=[ON_VMEM] * SIDE,
        out_shape=[jax.ShapeDtypeStruct(shape, jnp.bfloat16 if n else jnp.float32) for n in range(SIDE)],
        compiler_params=pltpu.CompilerParams(vmem_limit_bytes=16 * MIB),
        name="first_sum",
    )(table, *parts)


def second_sum_kernel(chunk, *refs):
    parts, own, handed = refs[:SIDE], refs[SIDE], refs[SIDE + 1]
    size, span = own.shape
    for n in range(len(chunk.held)):
        total = parts[0][:, n * size:(n + 1) * size]
        for part in parts[1:]:
            total = total + part[:, n * size:(n + 1) * size].astype(jnp.float32)
        if n * size < span:
            own[:, n * size:(n + 1) * size] = total
        if n in chunk.handed:
            handed[chunk.handed.index(n)] = total.T.astype(handed.dtype)


def second_sum(chunk, parts):
    size = parts[0].shape[0]
    return pl.pallas_call(
        functools.partial(second_sum_kernel, chunk),
        in_specs=[ON_VMEM] * SIDE,
        out_specs=[ON_VMEM] * 2,
        out_shape=[
            jax.ShapeDtypeStruct((size, len(chunk.steps) * size), jnp.float32),
            jax.ShapeDtypeStruct((len(chunk.handed), size, size), jnp.bfloat16),
        ],
        compiler_params=pltpu.CompilerParams(vmem_limit_bytes=16 * MIB),
        name="second_sum",
    )(*parts)


def place_kernel(at, table, *rest):
    owns, mirrors, out = rest[:len(CHUNKS)], rest[len(CHUNKS):-1], rest[-1]
    size = out.shape[0]

    def put(step, value):
        y = lax.rem(table[at.y] + step[0], SIDE)
        x = lax.rem(table[at.x] + step[1], SIDE)
        out[:, pl.ds(pl.multiple_of((y * SIDE + x) * size, size), size)] = value.astype(out.dtype)

    for chunk, own, mirror in zip(CHUNKS, owns, mirrors):
        for n, step in enumerate(chunk.steps):
            put(step, own[:, n * size:(n + 1) * size])
        for n, step in enumerate(chunk.arrivals()):
            put(step, mirror[n])


def place_blocks(at, table, owns, mirrors):
    size = owns[0].shape[0]
    return pl.pallas_call(
        functools.partial(place_kernel, at),
        in_specs=[ON_SMEM] + [ON_VMEM] * (len(owns) + len(mirrors)),
        out_specs=ON_VMEM,
        out_shape=jax.ShapeDtypeStruct((size, SIDE * SIDE * size), jnp.float32),
        compiler_params=pltpu.CompilerParams(vmem_limit_bytes=16 * MIB),
        name="place_blocks",
    )(table, *owns, *mirrors)


def along(axis, k):
    return functools.partial(lax.ppermute, axis_name=axis, perm=[(i, (i + k) % SIDE) for i in range(SIDE)])


def body(integrals, lam_index, tile_count, screen, coefficients, metric):
    at = Table(*integrals.shape[:2])
    place = jnp.stack([lax.axis_index(name).astype(jnp.int32) for name in ("core", "x", "y")])
    table = prepare(at, place, lam_index, tile_count, screen)
    same, other = gather(coefficients)
    mine = fit(at, table, integrals, same, other)
    fitted = lax.all_to_all(mine, ("y", "x"), 0, 0, tiled=True)
    factors, turned = factor(metric, fitted)

    def send(parts, axis):
        return [parts[0]] + [along(axis, k)(parts[k]) for k in (2, 1, 3)]

    panels = panel_columns(at, table, factors, turned)
    owns, mirrors = [], []
    for n, chunk in enumerate(CHUNKS):
        first, second = ("x", "y") if chunk.x_first else ("y", "x")
        sums = first_sum(at, chunk, table, send(panels[n * SIDE:(n + 1) * SIDE], first))
        own, handed = second_sum(chunk, send(sums, second))
        owns.append(own)
        mirrors.append(along(first, 1)(handed))
    return place_blocks(at, table, owns, mirrors)


def solution(mesh):
    pair, ri = ("z", "core"), ("y", "x")
    cores = 2
    devices = mesh.devices.reshape(mesh.shape["pair"] // cores, cores, SIDE, SIDE)
    named = jax.sharding.Mesh(devices, pair + ri)
    placed = (
        P(pair, None, ri, None, None),
        P(pair, None),
        P(pair),
        P(pair, None),
        P(None, pair + ri),
        P(),
    )
    return jax.shard_map(
        body, mesh=named, in_specs=placed, out_specs=P(pair + ri, None), check_vma=False
    )
```

```python
import functools

import jax
import jax.numpy as jnp
from jax import lax
from jax.experimental import pallas as pl
from jax.experimental.pallas import tpu as pltpu
from jax.sharding import PartitionSpec as P

MIB = 1024 * 1024
NT = (((1,), (1,)), ((), ()))
SIDE = 4
HALVES = 2
ON_VMEM = pl.BlockSpec(memory_space=pltpu.VMEM)
ON_SMEM = pl.BlockSpec(memory_space=pltpu.SMEM)
ANYWHERE = pl.BlockSpec(memory_space=pl.ANY)


class Chunk:
    def __init__(self, x_first, steps, hops, handed):
        self.x_first, self.steps, self.hops, self.handed = x_first, steps, hops, handed
        self.held = steps + [steps[n] for n, _ in hops]

    def arrivals(self):
        return [tuple(-d % SIDE for d in self.held[n]) for n in self.handed]


CHUNKS = (
    Chunk(False, [(0, 0), (1, 0), (1, 1), (1, 2), (1, 3)], [(2, 1), (3, 2), (4, 3)], [1, 5, 6, 7]),
    Chunk(True, [(0, 1), (0, 2), (2, 0), (2, 1), (2, 2)], [(3, 2)], [0, 5]),
)


class Table:
    def __init__(self, blocks, slots):
        self.blocks, self.slots = blocks, slots
        self.count = 0
        self.slot = self.count + blocks
        self.core = self.slot + blocks * slots
        self.name = self.core + blocks * slots
        self.x = self.name + blocks * slots
        self.y = self.x + 1
        self.size = self.y + 1


def prepare_kernel(at, place, lam, tile_count, screen, table):
    core = place[0]
    table[at.x] = place[1]
    table[at.y] = place[2]

    def one(b, _):
        count = jnp.int32(0)
        for s in range(at.slots):
            name = lam[s, b]
            to = b * at.slots + count
            table[at.slot + to] = s
            table[at.core + to] = ((name >> 4) ^ core) & 1
            table[at.name + to] = ((name >> 5) << 4) | (name & 15)
            keep = jnp.logical_and(s < tile_count[b], screen[s, b] > 0)
            count = count + keep.astype(jnp.int32)
        table[at.count + b] = count
        return 0

    lax.fori_loop(0, at.blocks, one, 0)


def prepare(at, place, lam, tile_count, screen):
    return pl.pallas_call(
        functools.partial(prepare_kernel, at),
        in_specs=[ON_SMEM] * 4,
        out_specs=ON_SMEM,
        out_shape=jax.ShapeDtypeStruct((at.size,), jnp.int32),
        name="prepare",
    )(place, lam.T, tile_count, screen.T)


def gather(coefficients):
    copies = jnp.broadcast_to(coefficients[None], (lax.axis_size(("z", "y", "x")),) + coefficients.shape)
    same = lax.all_to_all(copies, ("z", "y", "x"), 0, 0, tiled=True)
    return same, lax.ppermute(same, "core", [(0, 1), (1, 0)])


def fit_kernel(at, table, same, other, integrals, out, tiles, picked, total, done):
    slots = at.slots
    _, _, size = same.shape
    ri, steps, own_q, rows, _ = out.shape
    share = rows // HALVES

    def copy(block, j):
        slot = table[at.slot + block * slots + j]
        return pltpu.make_async_copy(integrals.at[block, slot], tiles.at[block, j], done.at[block, j])

    def kept(block, act):
        for j in range(slots):
            @pl.when(j < table[at.count + block])
            def _():
                act(copy(block, j))

    def begin(step, _):
        for half in range(HALVES):
            kept(step + half * steps, lambda c: c.start())
        return 0

    lax.fori_loop(0, steps, begin, 0)

    def one(step, _):
        for half in range(HALVES):
            block = step + half * steps
            count = table[at.count + block]
            kept(block, lambda c: c.wait())

            @pl.when(count == 0)
            def _():
                total[half] = jnp.zeros(total.shape[1:], total.dtype)

            for c in range(1, slots + 1):
                @pl.when(count == c)
                def _():
                    for j in range(c):
                        n = block * slots + j
                        name = table[at.name + n]
                        tile = jnp.where(table[at.core + n] == 0, same[name], other[name])
                        picked[half, :, j * size:(j + 1) * size] = tile
                    wide = [tiles[block, j].reshape(own_q * size, size) for j in range(c)]
                    wide = jnp.concatenate(wide, axis=1) if c > 1 else wide[0]
                    total[half] = lax.dot_general(
                        picked[half, :, :c * size], wide, NT, preferred_element_type=jnp.float32
                    )

        for q in range(own_q):
            parts = [
                total[half, :, q * size:(q + 1) * size].reshape(ri, share, size) for half in range(HALVES)
            ]
            out[:, step, q] = jnp.concatenate(parts, axis=1).astype(out.dtype)
        return 0

    lax.fori_loop(0, steps, one, 0)


def fit(at, table, integrals, same, other):
    blocks, slots, own_q, size, _ = integrals.shape
    occupied = same.shape[1]
    ri = SIDE * SIDE
    share = occupied // ri
    return pl.pallas_call(
        functools.partial(fit_kernel, at),
        in_specs=[ON_SMEM, ON_VMEM, ON_VMEM, ANYWHERE],
        out_specs=ON_VMEM,
        scratch_shapes=[
            pltpu.VMEM((blocks, slots, own_q, size, size), jnp.bfloat16),
            pltpu.VMEM((HALVES, occupied, slots * size), jnp.bfloat16),
            pltpu.VMEM((HALVES, occupied, own_q * size), jnp.float32),
            pltpu.SemaphoreType.DMA((blocks, slots)),
        ],
        out_shape=jax.ShapeDtypeStruct((ri, blocks // HALVES, own_q, HALVES * share, size), jnp.bfloat16),
        compiler_params=pltpu.CompilerParams(vmem_limit_bytes=40 * MIB),
        cost_estimate=pl.CostEstimate(flops=3 * 10 ** 9, bytes_accessed=20 * 10 ** 6, transcendentals=0),
        name="fit",
    )(table, same, other, integrals)


def factor_kernel(metric, fitted, factors, turned, wide):
    ri, steps, own_q, rows, tile = fitted.shape
    share = rows // HALVES
    n_q = metric.shape[0]
    lanes = wide.shape[1]
    chunk = lanes * tile
    half_cols = steps * tile

    def one(c, _):
        base = pl.multiple_of(c * chunk, chunk)
        for k in range(own_q):
            for t in range(lanes):
                x = fitted[:, c * lanes + t, k].astype(jnp.float32)
                for r in range(ri):
                    to = (r * own_q + k) * share
                    for h in range(HALVES):
                        wide[h, t, to:to + share, :] = x[r, h * share:(h + 1) * share]
        for h in range(HALVES):
            start = pl.multiple_of(base + h * half_cols, chunk)
            parts = []
            for o in range(share):
                x = jnp.concatenate(
                    [wide[h, t, pl.ds(o, n_q, stride=share), :] for t in range(lanes)], axis=1
                ).astype(jnp.bfloat16)
                parts.append(jnp.dot(metric[...], x, preferred_element_type=jnp.float32).astype(jnp.bfloat16))
            whole = jnp.concatenate(parts, axis=0)
            factors[:, pl.ds(start, chunk)] = whole
            turned[pl.ds(start, chunk), :] = whole.T
        return 0

    lax.fori_loop(0, steps // lanes, one, 0)


def factor(metric, fitted):
    ri, steps, own_q, rows, size = fitted.shape
    cols = HALVES * steps * size
    depth = own_q * ri * rows // HALVES
    return pl.pallas_call(
        factor_kernel,
        in_specs=[ON_VMEM] * 2,
        out_specs=[ON_VMEM] * 2,
        out_shape=[
            jax.ShapeDtypeStruct((depth, cols), jnp.bfloat16),
            jax.ShapeDtypeStruct((cols, depth), jnp.bfloat16),
        ],
        scratch_shapes=[pltpu.VMEM((HALVES, 2, depth, size), jnp.float32)],
        compiler_params=pltpu.CompilerParams(vmem_limit_bytes=20 * MIB),
        cost_estimate=pl.CostEstimate(flops=2 * 10 ** 9, bytes_accessed=10 * 10 ** 6, transcendentals=0),
        name="factor",
    )(metric, fitted)


def panel_kernel(at, table, factors, turned, *rest):
    outs, panels = rest[:-1], rest[-1]
    size = panels.shape[1]
    line = SIDE * size
    for k in range(SIDE):
        y = lax.rem(table[at.y] + k, SIDE)
        rows = turned[pl.ds(pl.multiple_of(y * line, line), line), :]
        for dy in sorted({dy for chunk in CHUNKS for dy, _ in chunk.steps}):
            start = pl.multiple_of(lax.rem(y + dy, SIDE) * line, line)
            value = jnp.dot(
                rows, factors[:, pl.ds(start, line)], preferred_element_type=jnp.float32
            ).astype(jnp.bfloat16)
            for n, chunk in enumerate(CHUNKS):
                for position, step in enumerate(chunk.steps):
                    if step[0] != dy:
                        continue
                    to = position * size
                    for x in range(SIDE):
                        col = (x + step[1]) % SIDE * size
                        block = value[x * size:(x + 1) * size, col:col + size]
                        if chunk.x_first:
                            panels[y * SIDE + x, :, to:to + size] = block
                        else:
                            outs[n * SIDE + k][x, :, to:to + size] = block
    for n, chunk in enumerate(CHUNKS):
        if chunk.x_first:
            for k in range(SIDE):
                x = lax.rem(table[at.x] + k, SIDE)
                for y in range(SIDE):
                    outs[n * SIDE + k][y] = panels[y * SIDE + x]


def panel_columns(at, table, factors, turned):
    cols, depth = turned.shape
    size = cols // (SIDE * SIDE)
    widest = max(len(chunk.steps) for chunk in CHUNKS if chunk.x_first) * size
    return pl.pallas_call(
        functools.partial(panel_kernel, at),
        in_specs=[ON_SMEM, ON_VMEM, ON_VMEM],
        out_specs=[ON_VMEM] * (len(CHUNKS) * SIDE),
        out_shape=[
            jax.ShapeDtypeStruct((SIDE, size, len(chunk.steps) * size), jnp.bfloat16)
            for chunk in CHUNKS
            for _ in range(SIDE)
        ],
        scratch_shapes=[pltpu.VMEM((SIDE * SIDE, size, widest), jnp.bfloat16)],
        compiler_params=pltpu.CompilerParams(vmem_limit_bytes=16 * MIB),
        cost_estimate=pl.CostEstimate(flops=8 * 10 ** 9, bytes_accessed=15 * 10 ** 6, transcendentals=0),
        name="panel_columns",
    )(table, factors, turned)


def first_sum_kernel(at, chunk, table, *rest):
    ins, outs = rest[:SIDE], rest[-SIDE:]
    size = outs[0].shape[0]
    own = len(chunk.steps) * size
    mine = table[at.y if chunk.x_first else at.x]

    def total(panel, start, stop):
        value = ins[0][panel, :, start:stop].astype(jnp.float32)
        for part in ins[1:]:
            value = value + part[panel, :, start:stop].astype(jnp.float32)
        return value

    for k, out in enumerate(outs):
        to = mine + k
        out[:, :own] = total(lax.rem(to, SIDE), 0, own).astype(out.dtype)
        for n, (position, back) in enumerate(chunk.hops):
            start = position * size
            value = total(lax.rem(to + SIDE - back, SIDE), start, start + size)
            out[:, own + n * size:own + (n + 1) * size] = value.astype(out.dtype)


def first_sum(at, chunk, table, parts):
    size = parts[0].shape[-2]
    shape = (size, len(chunk.held) * size)
    return pl.pallas_call(
        functools.partial(first_sum_kernel, at, chunk),
        in_specs=[ON_SMEM] + [ON_VMEM] * SIDE,
        out_specs=[ON_VMEM] * SIDE,
        out_shape=[jax.ShapeDtypeStruct(shape, jnp.bfloat16 if n else jnp.float32) for n in range(SIDE)],
        compiler_params=pltpu.CompilerParams(vmem_limit_bytes=16 * MIB),
        name="first_sum",
    )(table, *parts)


def second_sum_kernel(chunk, *refs):
    parts, own, handed = refs[:SIDE], refs[SIDE], refs[SIDE + 1]
    size, span = own.shape
    for n in range(len(chunk.held)):
        total = parts[0][:, n * size:(n + 1) * size]
        for part in parts[1:]:
            total = total + part[:, n * size:(n + 1) * size].astype(jnp.float32)
        if n * size < span:
            own[:, n * size:(n + 1) * size] = total
        if n in chunk.handed:
            handed[chunk.handed.index(n)] = total.T.astype(handed.dtype)


def second_sum(chunk, parts):
    size = parts[0].shape[0]
    return pl.pallas_call(
        functools.partial(second_sum_kernel, chunk),
        in_specs=[ON_VMEM] * SIDE,
        out_specs=[ON_VMEM] * 2,
        out_shape=[
            jax.ShapeDtypeStruct((size, len(chunk.steps) * size), jnp.float32),
            jax.ShapeDtypeStruct((len(chunk.handed), size, size), jnp.bfloat16),
        ],
        compiler_params=pltpu.CompilerParams(vmem_limit_bytes=16 * MIB),
        name="second_sum",
    )(*parts)


def place_kernel(at, table, *rest):
    owns, mirrors, out = rest[:len(CHUNKS)], rest[len(CHUNKS):-1], rest[-1]
    size = out.shape[0]

    def put(step, value):
        y = lax.rem(table[at.y] + step[0], SIDE)
        x = lax.rem(table[at.x] + step[1], SIDE)
        out[:, pl.ds(pl.multiple_of((y * SIDE + x) * size, size), size)] = value.astype(out.dtype)

    for chunk, own, mirror in zip(CHUNKS, owns, mirrors):
        for n, step in enumerate(chunk.steps):
            put(step, own[:, n * size:(n + 1) * size])
        for n, step in enumerate(chunk.arrivals()):
            put(step, mirror[n])


def place_blocks(at, table, owns, mirrors):
    size = owns[0].shape[0]
    return pl.pallas_call(
        functools.partial(place_kernel, at),
        in_specs=[ON_SMEM] + [ON_VMEM] * (len(owns) + len(mirrors)),
        out_specs=ON_VMEM,
        out_shape=jax.ShapeDtypeStruct((size, SIDE * SIDE * size), jnp.float32),
        compiler_params=pltpu.CompilerParams(vmem_limit_bytes=16 * MIB),
        name="place_blocks",
    )(table, *owns, *mirrors)


def along(axis, k):
    return functools.partial(lax.ppermute, axis_name=axis, perm=[(i, (i + k) % SIDE) for i in range(SIDE)])


def body(integrals, lam_index, tile_count, screen, coefficients, metric):
    at = Table(*integrals.shape[:2])
    place = jnp.stack([lax.axis_index(name).astype(jnp.int32) for name in ("core", "x", "y")])
    table = prepare(at, place, lam_index, tile_count, screen)
    same, other = gather(coefficients)
    mine = fit(at, table, integrals, same, other)
    fitted = lax.all_to_all(mine, ("y", "x"), 0, 0, tiled=True)
    factors, turned = factor(metric, fitted)

    def send(parts, axis):
        return [parts[0]] + [along(axis, k)(parts[k]) for k in (2, 1, 3)]

    panels = panel_columns(at, table, factors, turned)
    owns, mirrors = [], []
    for n, chunk in enumerate(CHUNKS):
        first, second = ("x", "y") if chunk.x_first else ("y", "x")
        sums = first_sum(at, chunk, table, send(panels[n * SIDE:(n + 1) * SIDE], first))
        own, handed = second_sum(chunk, send(sums, second))
        owns.append(own)
        mirrors.append(along(first, 1)(handed))
    return place_blocks(at, table, owns, mirrors)


def solution(mesh):
    pair, ri = ("z", "core"), ("y", "x")
    cores = 2
    devices = mesh.devices.reshape(mesh.shape["pair"] // cores, cores, SIDE, SIDE)
    named = jax.sharding.Mesh(devices, pair + ri)
    placed = (
        P(pair, None, ri, None, None),
        P(pair, None),
        P(pair),
        P(pair, None),
        P(None, pair + ri),
        P(),
    )
    return jax.shard_map(
        body, mesh=named, in_specs=placed, out_specs=P(pair + ri, None), check_vma=False
    )
```

```python
import functools

import jax
import jax.numpy as jnp
from jax import lax
from jax.experimental import pallas as pl
from jax.experimental.pallas import tpu as pltpu
from jax.sharding import PartitionSpec as P

MIB = 1024 * 1024
NT = (((1,), (1,)), ((), ()))
SIDE = 4
HALVES = 2
ON_VMEM = pl.BlockSpec(memory_space=pltpu.VMEM)
ON_SMEM = pl.BlockSpec(memory_space=pltpu.SMEM)
ANYWHERE = pl.BlockSpec(memory_space=pl.ANY)


class Chunk:
    def __init__(self, x_first, steps, hops, handed):
        self.x_first, self.steps, self.hops, self.handed = x_first, steps, hops, handed
        self.held = steps + [steps[n] for n, _ in hops]

    def arrivals(self):
        return [tuple(-d % SIDE for d in self.held[n]) for n in self.handed]


CHUNKS = (
    Chunk(False, [(0, 0), (1, 0), (1, 1), (1, 2), (1, 3)], [(2, 1), (3, 2), (4, 3)], [1, 5, 6, 7]),
    Chunk(True, [(0, 1), (0, 2), (2, 0), (2, 1), (2, 2)], [(3, 2)], [0, 5]),
)


class Table:
    def __init__(self, blocks, slots):
        self.blocks, self.slots = blocks, slots
        self.count = 0
        self.slot = self.count + blocks
        self.core = self.slot + blocks * slots
        self.name = self.core + blocks * slots
        self.x = self.name + blocks * slots
        self.y = self.x + 1
        self.size = self.y + 1


def prepare_kernel(at, place, lam, tile_count, screen, table):
    core = place[0]
    table[at.x] = place[1]
    table[at.y] = place[2]

    def one(b, _):
        count = jnp.int32(0)
        for s in range(at.slots):
            name = lam[s, b]
            to = b * at.slots + count
            table[at.slot + to] = s
            table[at.core + to] = ((name >> 4) ^ core) & 1
            table[at.name + to] = ((name >> 5) << 4) | (name & 15)
            keep = jnp.logical_and(s < tile_count[b], screen[s, b] > 0)
            count = count + keep.astype(jnp.int32)
        table[at.count + b] = count
        return 0

    lax.fori_loop(0, at.blocks, one, 0)


def prepare(at, place, lam, tile_count, screen):
    return pl.pallas_call(
        functools.partial(prepare_kernel, at),
        in_specs=[ON_SMEM] * 4,
        out_specs=ON_SMEM,
        out_shape=jax.ShapeDtypeStruct((at.size,), jnp.int32),
        name="prepare",
    )(place, lam.T, tile_count, screen.T)


def gather(coefficients):
    copies = jnp.broadcast_to(coefficients[None], (lax.axis_size(("z", "y", "x")),) + coefficients.shape)
    same = lax.all_to_all(copies, ("z", "y", "x"), 0, 0, tiled=True)
    return same, lax.ppermute(same, "core", [(0, 1), (1, 0)])


def fit_kernel(at, table, same, other_core, integrals, out, tiles, others, picked, total, done, arrived):
    slots = at.slots
    _, _, size = same.shape
    ri, steps, own_q, rows, _ = out.shape
    share = rows // HALVES

    def copy(block, j):
        slot = table[at.slot + block * slots + j]
        return pltpu.make_async_copy(integrals.at[block, slot], tiles.at[block, j], done.at[block, j])

    def kept(block, act):
        for j in range(slots):
            @pl.when(j < table[at.count + block])
            def _():
                act(copy(block, j))

    def begin(step, _):
        for half in range(HALVES):
            kept(step + half * steps, lambda c: c.start())
        return 0

    swap = pltpu.make_async_copy(other_core, others, arrived)
    swap.start()
    lax.fori_loop(0, steps, begin, 0)
    swap.wait()

    def one(step, _):
        for half in range(HALVES):
            block = step + half * steps
            count = table[at.count + block]
            kept(block, lambda c: c.wait())

            @pl.when(count == 0)
            def _():
                total[half] = jnp.zeros(total.shape[1:], total.dtype)

            for c in range(1, slots + 1):
                @pl.when(count == c)
                def _():
                    for j in range(c):
                        n = block * slots + j
                        name = table[at.name + n]
                        tile = jnp.where(table[at.core + n] == 0, same[name], others[name])
                        picked[half, :, j * size:(j + 1) * size] = tile
                    wide = [tiles[block, j].reshape(own_q * size, size) for j in range(c)]
                    wide = jnp.concatenate(wide, axis=1) if c > 1 else wide[0]
                    total[half] = lax.dot_general(
                        picked[half, :, :c * size], wide, NT, preferred_element_type=jnp.float32
                    )

        for q in range(own_q):
            parts = [
                total[half, :, q * size:(q + 1) * size].reshape(ri, share, size) for half in range(HALVES)
            ]
            out[:, step, q] = jnp.concatenate(parts, axis=1).astype(out.dtype)
        return 0

    lax.fori_loop(0, steps, one, 0)


def fit(at, table, integrals, same, other):
    blocks, slots, own_q, size, _ = integrals.shape
    occupied = same.shape[1]
    ri = SIDE * SIDE
    share = occupied // ri
    return pl.pallas_call(
        functools.partial(fit_kernel, at),
        in_specs=[ON_SMEM, ON_VMEM, ANYWHERE, ANYWHERE],
        out_specs=ON_VMEM,
        scratch_shapes=[
            pltpu.VMEM((blocks, slots, own_q, size, size), jnp.bfloat16),
            pltpu.VMEM(other.shape, jnp.bfloat16),
            pltpu.VMEM((HALVES, occupied, slots * size), jnp.bfloat16),
            pltpu.VMEM((HALVES, occupied, own_q * size), jnp.float32),
            pltpu.SemaphoreType.DMA((blocks, slots)),
            pltpu.SemaphoreType.DMA,
        ],
        out_shape=jax.ShapeDtypeStruct((ri, blocks // HALVES, own_q, HALVES * share, size), jnp.bfloat16),
        compiler_params=pltpu.CompilerParams(vmem_limit_bytes=40 * MIB),
        cost_estimate=pl.CostEstimate(flops=3 * 10 ** 9, bytes_accessed=20 * 10 ** 6, transcendentals=0),
        name="fit",
    )(table, same, other, integrals)


def factor_kernel(metric, fitted, factors, turned, wide):
    ri, steps, own_q, rows, tile = fitted.shape
    share = rows // HALVES
    n_q = metric.shape[0]
    lanes = wide.shape[1]
    chunk = lanes * tile
    half_cols = steps * tile

    def one(c, _):
        base = pl.multiple_of(c * chunk, chunk)
        for k in range(own_q):
            for t in range(lanes):
                x = fitted[:, c * lanes + t, k].astype(jnp.float32)
                for r in range(ri):
                    to = (r * own_q + k) * share
                    for h in range(HALVES):
                        wide[h, t, to:to + share, :] = x[r, h * share:(h + 1) * share]
        for h in range(HALVES):
            start = pl.multiple_of(base + h * half_cols, chunk)
            parts = []
            for o in range(share):
                x = jnp.concatenate(
                    [wide[h, t, pl.ds(o, n_q, stride=share), :] for t in range(lanes)], axis=1
                ).astype(jnp.bfloat16)
                parts.append(jnp.dot(metric[...], x, preferred_element_type=jnp.float32).astype(jnp.bfloat16))
            whole = jnp.concatenate(parts, axis=0)
            factors[:, pl.ds(start, chunk)] = whole
            turned[pl.ds(start, chunk), :] = whole.T
        return 0

    lax.fori_loop(0, steps // lanes, one, 0)


def factor(metric, fitted):
    ri, steps, own_q, rows, size = fitted.shape
    cols = HALVES * steps * size
    depth = own_q * ri * rows // HALVES
    return pl.pallas_call(
        factor_kernel,
        in_specs=[ON_VMEM] * 2,
        out_specs=[ON_VMEM] * 2,
        out_shape=[
            jax.ShapeDtypeStruct((depth, cols), jnp.bfloat16),
            jax.ShapeDtypeStruct((cols, depth), jnp.bfloat16),
        ],
        scratch_shapes=[pltpu.VMEM((HALVES, 2, depth, size), jnp.float32)],
        compiler_params=pltpu.CompilerParams(vmem_limit_bytes=20 * MIB),
        cost_estimate=pl.CostEstimate(flops=2 * 10 ** 9, bytes_accessed=10 * 10 ** 6, transcendentals=0),
        name="factor",
    )(metric, fitted)


def panel_kernel(at, table, factors, turned, *rest):
    outs, panels = rest[:-1], rest[-1]
    size = panels.shape[1]
    line = SIDE * size
    for k in range(SIDE):
        y = lax.rem(table[at.y] + k, SIDE)
        rows = turned[pl.ds(pl.multiple_of(y * line, line), line), :]
        for dy in sorted({dy for chunk in CHUNKS for dy, _ in chunk.steps}):
            start = pl.multiple_of(lax.rem(y + dy, SIDE) * line, line)
            value = jnp.dot(
                rows, factors[:, pl.ds(start, line)], preferred_element_type=jnp.float32
            ).astype(jnp.bfloat16)
            for n, chunk in enumerate(CHUNKS):
                for position, step in enumerate(chunk.steps):
                    if step[0] != dy:
                        continue
                    to = position * size
                    for x in range(SIDE):
                        col = (x + step[1]) % SIDE * size
                        block = value[x * size:(x + 1) * size, col:col + size]
                        if chunk.x_first:
                            panels[y * SIDE + x, :, to:to + size] = block
                        else:
                            outs[n * SIDE + k][x, :, to:to + size] = block
    for n, chunk in enumerate(CHUNKS):
        if chunk.x_first:
            for k in range(SIDE):
                x = lax.rem(table[at.x] + k, SIDE)
                for y in range(SIDE):
                    outs[n * SIDE + k][y] = panels[y * SIDE + x]


def panel_columns(at, table, factors, turned):
    cols, depth = turned.shape
    size = cols // (SIDE * SIDE)
    widest = max(len(chunk.steps) for chunk in CHUNKS if chunk.x_first) * size
    return pl.pallas_call(
        functools.partial(panel_kernel, at),
        in_specs=[ON_SMEM, ON_VMEM, ON_VMEM],
        out_specs=[ON_VMEM] * (len(CHUNKS) * SIDE),
        out_shape=[
            jax.ShapeDtypeStruct((SIDE, size, len(chunk.steps) * size), jnp.bfloat16)
            for chunk in CHUNKS
            for _ in range(SIDE)
        ],
        scratch_shapes=[pltpu.VMEM((SIDE * SIDE, size, widest), jnp.bfloat16)],
        compiler_params=pltpu.CompilerParams(vmem_limit_bytes=16 * MIB),
        cost_estimate=pl.CostEstimate(flops=8 * 10 ** 9, bytes_accessed=15 * 10 ** 6, transcendentals=0),
        name="panel_columns",
    )(table, factors, turned)


def first_sum_kernel(at, chunk, table, *rest):
    ins, outs = rest[:SIDE], rest[-SIDE:]
    size = outs[0].shape[0]
    own = len(chunk.steps) * size
    mine = table[at.y if chunk.x_first else at.x]

    def total(panel, start, stop):
        value = ins[0][panel, :, start:stop].astype(jnp.float32)
        for part in ins[1:]:
            value = value + part[panel, :, start:stop].astype(jnp.float32)
        return value

    for k, out in enumerate(outs):
        to = mine + k
        out[:, :own] = total(lax.rem(to, SIDE), 0, own).astype(out.dtype)
        for n, (position, back) in enumerate(chunk.hops):
            start = position * size
            value = total(lax.rem(to + SIDE - back, SIDE), start, start + size)
            out[:, own + n * size:own + (n + 1) * size] = value.astype(out.dtype)


def first_sum(at, chunk, table, parts):
    size = parts[0].shape[-2]
    shape = (size, len(chunk.held) * size)
    return pl.pallas_call(
        functools.partial(first_sum_kernel, at, chunk),
        in_specs=[ON_SMEM] + [ON_VMEM] * SIDE,
        out_specs=[ON_VMEM] * SIDE,
        out_shape=[jax.ShapeDtypeStruct(shape, jnp.bfloat16 if n else jnp.float32) for n in range(SIDE)],
        compiler_params=pltpu.CompilerParams(vmem_limit_bytes=16 * MIB),
        name="first_sum",
    )(table, *parts)


def second_sum_kernel(chunk, *refs):
    parts, own, handed = refs[:SIDE], refs[SIDE], refs[SIDE + 1]
    size, span = own.shape
    for n in range(len(chunk.held)):
        total = parts[0][:, n * size:(n + 1) * size]
        for part in parts[1:]:
            total = total + part[:, n * size:(n + 1) * size].astype(jnp.float32)
        if n * size < span:
            own[:, n * size:(n + 1) * size] = total
        if n in chunk.handed:
            handed[chunk.handed.index(n)] = total.T.astype(handed.dtype)


def second_sum(chunk, parts):
    size = parts[0].shape[0]
    return pl.pallas_call(
        functools.partial(second_sum_kernel, chunk),
        in_specs=[ON_VMEM] * SIDE,
        out_specs=[ON_VMEM] * 2,
        out_shape=[
            jax.ShapeDtypeStruct((size, len(chunk.steps) * size), jnp.float32),
            jax.ShapeDtypeStruct((len(chunk.handed), size, size), jnp.bfloat16),
        ],
        compiler_params=pltpu.CompilerParams(vmem_limit_bytes=16 * MIB),
        name="second_sum",
    )(*parts)


def place_kernel(at, table, *rest):
    owns, mirrors, out = rest[:len(CHUNKS)], rest[len(CHUNKS):-1], rest[-1]
    size = out.shape[0]

    def put(step, value):
        y = lax.rem(table[at.y] + step[0], SIDE)
        x = lax.rem(table[at.x] + step[1], SIDE)
        out[:, pl.ds(pl.multiple_of((y * SIDE + x) * size, size), size)] = value.astype(out.dtype)

    for chunk, own, mirror in zip(CHUNKS, owns, mirrors):
        for n, step in enumerate(chunk.steps):
            put(step, own[:, n * size:(n + 1) * size])
        for n, step in enumerate(chunk.arrivals()):
            put(step, mirror[n])


def place_blocks(at, table, owns, mirrors):
    size = owns[0].shape[0]
    return pl.pallas_call(
        functools.partial(place_kernel, at),
        in_specs=[ON_SMEM] + [ON_VMEM] * (len(owns) + len(mirrors)),
        out_specs=ON_VMEM,
        out_shape=jax.ShapeDtypeStruct((size, SIDE * SIDE * size), jnp.float32),
        compiler_params=pltpu.CompilerParams(vmem_limit_bytes=16 * MIB),
        name="place_blocks",
    )(table, *owns, *mirrors)


def along(axis, k):
    return functools.partial(lax.ppermute, axis_name=axis, perm=[(i, (i + k) % SIDE) for i in range(SIDE)])


def body(integrals, lam_index, tile_count, screen, coefficients, metric):
    at = Table(*integrals.shape[:2])
    place = jnp.stack([lax.axis_index(name).astype(jnp.int32) for name in ("core", "x", "y")])
    table = prepare(at, place, lam_index, tile_count, screen)
    same, other = gather(coefficients)
    mine = fit(at, table, integrals, same, other)
    fitted = lax.all_to_all(mine, ("y", "x"), 0, 0, tiled=True)
    factors, turned = factor(metric, fitted)

    def send(parts, axis):
        return [parts[0]] + [along(axis, k)(parts[k]) for k in (2, 1, 3)]

    panels = panel_columns(at, table, factors, turned)
    owns, mirrors = [], []
    for n, chunk in enumerate(CHUNKS):
        first, second = ("x", "y") if chunk.x_first else ("y", "x")
        sums = first_sum(at, chunk, table, send(panels[n * SIDE:(n + 1) * SIDE], first))
        own, handed = second_sum(chunk, send(sums, second))
        owns.append(own)
        mirrors.append(along(first, 1)(handed))
    return place_blocks(at, table, owns, mirrors)


def solution(mesh):
    pair, ri = ("z", "core"), ("y", "x")
    cores = 2
    devices = mesh.devices.reshape(mesh.shape["pair"] // cores, cores, SIDE, SIDE)
    named = jax.sharding.Mesh(devices, pair + ri)
    placed = (
        P(pair, None, ri, None, None),
        P(pair, None),
        P(pair),
        P(pair, None),
        P(None, pair + ri),
        P(),
    )
    return jax.shard_map(
        body, mesh=named, in_specs=placed, out_specs=P(pair + ri, None), check_vma=False
    )
```
